256 devices in a mesh: lat: 16 (over y, x_hi, core), lon: 16 (over x_lo, z).
Axes of the slice: x: 4 (x_hi: 2, x_lo: 2; x = x_hi * 2 + x_lo), y: 4, z: 8, core: 2. Of those that a mesh axis runs over, the one named last changes fastest.
Arguments:
- inputs: bfloat16 [2, 96, 192, 384], P(None, 'lat', 'lon'), may hold values from -6 to 6
- cotangent: bfloat16 [2, 96, 192, 384], P(None, 'lat', 'lon'), may hold values from -6 to 6
- norm_gain: float32 [384], replicated, may hold values from 0.1 to 1.9
- qkv_weight: bfloat16 [384, 1152], replicated, may hold values from -8 to 8
- proj_weight: bfloat16 [384, 384], replicated, may hold values from -0.3125 to 0.3125
- bias_table: bfloat16 [32, 12, 3312], replicated, may hold values from -4 to 320
- window_type: int32 [16, 1], P('lat'), may hold values from 0 to 31
- region: int32 [2, 96, 192], P(None, 'lat', 'lon'), may hold values from 0 to 2
Outputs:
- block_out: bfloat16 [2, 96, 192, 384], P(None, 'lat', 'lon')
- grad_inputs: bfloat16 [2, 96, 192, 384], P(None, 'lat', 'lon')
- grad_gain: float32 [384], replicated
- grad_qkv: float32 [384, 1152], P('lat', 'lon')
- grad_proj: float32 [384, 384], P('lat', 'lon')
- grad_bias: float32 [32, 12, 3312], P('lat', None, 'lon')
The draws below stay inside these ranges and needn't reach their ends.
All inputs are finite; a program needn't handle non-finite values.
Results may differ from the reference program's by a relative error of at most 0.0088.
Values may be sent and summed in bfloat16 or wider, within the bound.
A program may use at most 128 MiB of HBM per device.

```python
import jax
import jax.numpy as jnp
import numpy as np
from jax import lax

D = 384
HEADS = 12
LEV = 2
TYPES = 32
REL = 3312
LAT = 96
LON = 192


def draw_qkv_weight(key, part):
    key = jax.random.fold_in(key, 11)
    normal_key = jax.random.fold_in(key, 0)
    base_draw = jnp.clip(jax.random.normal(normal_key, (D, 3 * D), jnp.float32), -4.0, 4.0) * D ** (-0.5)
    return base_draw.astype(jnp.bfloat16)


def draw_bias_table(key, part):
    key = jax.random.fold_in(key, 23)
    normal_key = jax.random.fold_in(key, 0)
    base_draw = jnp.clip(jax.random.normal(normal_key, (TYPES, HEADS, REL), jnp.float32), -4.0, 4.0)
    return base_draw.astype(jnp.bfloat16)


def set_ends(entries, own_key, least, largest):
    spot = [jax.random.randint(jax.random.fold_in(own_key, axis), (), 0, length) for axis, length in enumerate(entries.shape)]
    widest = entries.shape.index(max(entries.shape))
    neighbour = spot[:widest] + [(spot[widest] + 1) % entries.shape[widest]] + spot[widest + 1:]
    return entries.at[tuple(spot)].set(least).at[tuple(neighbour)].set(largest)


def shard_levels(key, shape, cuts, low, largest):
    loudness = 1.0
    for position, parts in cuts:
        heights = jax.random.uniform(jax.random.fold_in(jax.random.fold_in(key, 6), position), (parts,), jnp.float32, low / len(cuts), largest / len(cuts))
        loudness = loudness * jnp.repeat(jnp.exp(heights), shape[position] // parts).reshape((-1,) + (1,) * (len(shape) - 1 - position))
    return loudness


def gaussian(own_key, dims, deviation, reach, cuts=(), kind=jnp.bfloat16):
    entries = jax.random.normal(own_key, dims, jnp.float32) * deviation
    if len(cuts) > 0:
        entries = shard_levels(own_key, dims, cuts, -0.22, 0.18) * entries
    return jnp.clip(entries, min=-reach, max=reach).astype(kind)


def setup_inputs(seed: int = 0) -> dict:
    streams_of = jax.random.split(jax.random.key(seed), 9)
    return {
        "inputs": gaussian(streams_of[0], (LEV, LAT, LON, D), 1.0, 6.0, ((1, 16), (2, 16))),
        "cotangent": gaussian(streams_of[1], (LEV, LAT, LON, D), 1.0, 6.0, ((1, 16), (2, 16))),
        "norm_gain": jnp.clip(1.0 + 0.18 * jax.random.normal(streams_of[2], (D,), jnp.float32), 0.1, 1.9),
        "qkv_weight": draw_qkv_weight(jax.random.fold_in(streams_of[8], 71), 0),
        "proj_weight": gaussian(streams_of[4], (D, D), D ** -0.5, 0.3125),
        "bias_table": draw_bias_table(jax.random.fold_in(streams_of[8], 71), 0),
        "window_type": set_ends(jax.random.randint(streams_of[6], (LAT // 6, LEV // 2), 0, TYPES), jax.random.fold_in(streams_of[6], 1), 0, TYPES - 1).astype(jnp.int32),
        "region": set_ends(jax.random.randint(streams_of[7], (LEV, LAT, LON), 0, 3), jax.random.fold_in(streams_of[7], 1), 0, 2).astype(jnp.int32),
    }


def relative_index():
    level_pos, row_pos, col_pos = np.meshgrid(np.arange(2), np.arange(6), np.arange(12), indexing='ij')
    level_pos = level_pos.reshape(-1)
    row_pos = row_pos.reshape(-1)
    col_pos = col_pos.reshape(-1)
    pair_level = level_pos[:, None] * 2 + level_pos[None, :]
    pair_row = row_pos[:, None] * 6 + row_pos[None, :]
    offset = col_pos[:, None] - col_pos[None, :] + 11
    return jnp.asarray(((pair_level * 36 + pair_row) * 23 + offset).astype(np.int32))

def to_windows(block_in):
    levels, row_count, col_count, feature_count = block_in.shape
    tiled_grid = block_in.reshape(levels // 2, 2, row_count // 6, 6, col_count // 12, 12, feature_count)
    tiled_grid = tiled_grid.transpose(0, 2, 4, 1, 3, 5, 6)
    return tiled_grid.reshape(-1, 144, feature_count)

def from_windows(windows, levels, row_count, col_count):
    feature_count = windows.shape[-1]
    tiled_grid = windows.reshape(levels // 2, row_count // 6, col_count // 12, 2, 6, 12, feature_count)
    return tiled_grid.transpose(0, 3, 1, 4, 2, 5, 6).reshape(levels, row_count, col_count, feature_count)

def product(pattern, left_op, right_op):
    return jnp.einsum(pattern, left_op.astype(jnp.float32), right_op.astype(jnp.float32), precision=lax.Precision.HIGHEST)

def window_pass(inputs, cotangent, cell_key, norm_gain, qkv_weight, proj_weight, bias_rows):
    win_count, tokens_win, model_width = inputs.shape
    head_count = bias_rows.shape[1]
    head_dim = model_width // head_count
    score_scale = head_dim ** (-0.5)
    wide_in = inputs.reshape(-1, model_width).astype(jnp.float32)
    center = lax.optimization_barrier(jnp.mean(wide_in, -1, keepdims=True))
    spread = lax.optimization_barrier(jnp.mean(jnp.square(wide_in - center), -1, keepdims=True))
    inv_std = lax.rsqrt(spread + 1e-05)
    normed = (wide_in - center) * inv_std
    hidden = (normed * norm_gain).astype(jnp.bfloat16)
    joined_qkv = jnp.dot(hidden, qkv_weight, preferred_element_type=jnp.float32).astype(jnp.bfloat16)
    joined_qkv = joined_qkv.reshape(win_count, tokens_win, 3, head_count, head_dim)
    queries = joined_qkv[:, :, 0]
    key_rows = joined_qkv[:, :, 1]
    value_rows = joined_qkv[:, :, 2]
    rel_table = relative_index()
    bias_full = jnp.take(bias_rows, rel_table, axis=2)
    scores = product('wqhd,wkhd->whqk', queries, key_rows) * score_scale + bias_full
    allowed = (cell_key[:, :, None] == cell_key[:, None, :])[:, None]
    scores = jnp.where(allowed, scores, -1e+30)
    row_top = lax.optimization_barrier(jnp.max(scores, -1, keepdims=True))
    exp_scores = jnp.exp(scores - row_top)
    probs_full = exp_scores / lax.optimization_barrier(jnp.sum(exp_scores, -1, keepdims=True))
    probs_low = probs_full.astype(jnp.bfloat16)
    attended = product('whqk,wkhd->wqhd', probs_low, value_rows).astype(jnp.bfloat16).reshape(-1, model_width)
    branch = jnp.dot(attended, proj_weight, preferred_element_type=jnp.float32)
    result = (wide_in + branch).astype(jnp.bfloat16)
    grad_flat = cotangent.reshape(-1, model_width)
    grad_proj = jnp.dot(attended.T, grad_flat, preferred_element_type=jnp.float32)
    grad_att = jnp.dot(grad_flat, proj_weight.T, preferred_element_type=jnp.float32).astype(jnp.bfloat16)
    grad_att = grad_att.reshape(win_count, tokens_win, head_count, head_dim)
    grad_probs = product('wqhd,wkhd->whqk', grad_att, value_rows)
    grad_values = product('whqk,wqhd->wkhd', probs_low, grad_att)
    grad_scores = probs_full * (grad_probs - lax.optimization_barrier(jnp.sum(probs_full * grad_probs, -1, keepdims=True)))
    pair_terms = grad_scores.reshape(win_count * head_count, tokens_win * tokens_win).T
    grad_bias = jax.ops.segment_sum(pair_terms, rel_table.reshape(-1), num_segments=bias_rows.shape[2])
    grad_bias = grad_bias.T.reshape(win_count, head_count, bias_rows.shape[2])
    grad_scaled = (grad_scores * score_scale).astype(jnp.bfloat16)
    grad_query = product('whqk,wkhd->wqhd', grad_scaled, key_rows)
    grad_keys = product('whqk,wqhd->wkhd', grad_scaled, queries)
    grad_joined = jnp.stack([grad_query, grad_keys, grad_values], 2).astype(jnp.bfloat16).reshape(-1, 3 * model_width)
    grad_qkv = jnp.dot(hidden.T, grad_joined, preferred_element_type=jnp.float32)
    grad_hidden = jnp.dot(grad_joined, qkv_weight.T, preferred_element_type=jnp.float32)
    grad_gain = lax.optimization_barrier(jnp.sum(grad_hidden * normed, 0))
    grad_normed = grad_hidden * norm_gain
    grad_wide = inv_std * (grad_normed - lax.optimization_barrier(jnp.mean(grad_normed, -1, keepdims=True)) - normed * lax.optimization_barrier(jnp.mean(grad_normed * normed, -1, keepdims=True)))
    grad_in = (grad_flat.astype(jnp.float32) + grad_wide).astype(jnp.bfloat16)
    return (result.reshape(inputs.shape), grad_in.reshape(inputs.shape), grad_qkv, grad_proj, grad_gain, grad_bias)

def reference(inputs, cotangent, norm_gain, qkv_weight, proj_weight, bias_table, window_type, region):
    levels, lat_total, lon_total, model_width = inputs.shape
    rolled = jnp.roll(inputs, (-1, -3, -6), axis=(0, 1, 2))
    rolled_cot = jnp.roll(cotangent, (-1, -3, -6), axis=(0, 1, 2))
    row_ids = jnp.arange(lat_total, dtype=jnp.int32)
    level_ids = jnp.arange(levels, dtype=jnp.int32)
    lat_side = (row_ids + 3 >= lat_total).astype(jnp.int32)
    lev_side = (level_ids + 1 >= levels).astype(jnp.int32)
    key_grid = region * 4 + lat_side[None, :, None] * 2 + lev_side[:, None, None]
    band_count = lat_total // 6
    head_count = bias_table.shape[1]

    def one_band(totals, band_index):
        band_start = (band_index * 6).astype(jnp.int32)
        block_in = lax.dynamic_slice_in_dim(rolled, band_start, 6, 1)
        block_cot = lax.dynamic_slice_in_dim(rolled_cot, band_start, 6, 1)
        block_key = lax.dynamic_slice_in_dim(key_grid, band_start, 6, 1)
        type_rows = lax.dynamic_index_in_dim(window_type, band_index, 0, keepdims=False)
        per_window = jnp.repeat(type_rows, lon_total // 12)
        bias_rows = bias_table[per_window].astype(jnp.float32)
        pieces = window_pass(to_windows(block_in), to_windows(block_cot), to_windows(block_key[..., None])[..., 0], norm_gain, qkv_weight, proj_weight, bias_rows)
        result_win, grad_win, grad_qkv, grad_proj, grad_gain, grad_bias_win = pieces
        sum_qkv, sum_proj, sum_gain, sum_bias = totals
        sum_bias = sum_bias.at[per_window].add(grad_bias_win)
        totals = (sum_qkv + grad_qkv, sum_proj + grad_proj, sum_gain + grad_gain, sum_bias)
        return (totals, (from_windows(result_win, levels, 6, lon_total), from_windows(grad_win, levels, 6, lon_total)))
    start_totals = (jnp.zeros((model_width, 3 * model_width), jnp.float32), jnp.zeros((model_width, model_width), jnp.float32), jnp.zeros((model_width,), jnp.float32), jnp.zeros(bias_table.shape, jnp.float32))
    totals, blocks = lax.scan(one_band, start_totals, jnp.arange(band_count, dtype=jnp.int32))
    result_blocks, grad_blocks = blocks
    block_out = result_blocks.transpose(1, 0, 2, 3, 4).reshape(levels, lat_total, lon_total, model_width)
    grad_inputs = grad_blocks.transpose(1, 0, 2, 3, 4).reshape(levels, lat_total, lon_total, model_width)
    block_out = jnp.roll(block_out, (1, 3, 6), axis=(0, 1, 2))
    grad_inputs = jnp.roll(grad_inputs, (1, 3, 6), axis=(0, 1, 2))
    sum_qkv, sum_proj, sum_gain, sum_bias = totals
    return (block_out, grad_inputs, sum_gain, sum_qkv, sum_proj, sum_bias)
```

```python
import functools

import jax
import jax.numpy as jnp
import numpy as np
from jax import lax
from jax.experimental import pallas as pl
from jax.experimental.pallas import tpu as pltpu
from jax.sharding import PartitionSpec as P

F32 = jnp.float32
BF16 = jnp.bfloat16
MESH = pl.DeviceIdType.MESH
SCALE = 32 ** (-0.5)


def patterns():
    pack = np.zeros((320, 384), np.float32)
    order = np.zeros((288, 320), np.float32)
    toeplitz = np.zeros((6, 1024, 144), np.float32)
    dup = np.zeros((2, 288, 192), np.float32)
    key_rows = np.zeros((144, 16), np.float32)
    key_cols = np.zeros((144, 128), np.float32)
    halves = np.zeros((384, 512), np.float32)
    for l in range(2):
        for r in range(6):
            for c in range(12):
                p = 12 * c + 6 * l + r
                quad = 2 * (r // 3) + c // 6
                t = (l * 3 + r % 3) * 6 + c % 6
                slab = 16 * (6 * l + r) + c
                pack[80 * quad + t, slab] = 1
                pack[80 * quad + 36 + t, 192 + slab] = 1
                order[p, 80 * quad + t] = 1
                order[144 + p, 80 * quad + 36 + t] = 1
                key_rows[p, 8 * (1 - l) + (r + 3) % 6] = 1
                key_cols[p, (c + 6) % 12] = 1
                for m in range(6):
                    for par in range(2):
                        spot = (2 * m + par + 6) % 12 - (c + 6) % 12 + 11
                        iq = (r + 3) % 6
                        lane = ((1 - l) * 2 + iq // 3) * 128 + (iq % 3) * 23 + spot
                        toeplitz[m, 512 * par + lane, p] = 1
    for h in range(12):
        for par in range(2):
            for l in range(2):
                for r in range(6):
                    zi = (1 - l) * 6 + (r + 3) % 6
                    dup[par, 24 * h + 12 * par + 6 * l + r, 16 * zi + h] = 1
    for f in range(384):
        i = f // 24
        halves[f, 256 * (i % 2) + 24 * (i // 2) + f % 24] = 1
    both = [
        pack,
        pack.T,
        order,
        order.T,
        toeplitz,
        dup,
        dup.transpose(0, 2, 1),
        key_rows,
        key_cols,
        key_cols.T,
        halves,
    ]
    return [jnp.asarray(x, BF16) for x in both]


def dot(a, b, ca=1, cb=0):
    return lax.dot_general(a, b, (((ca,), (cb,)), ((), ())), preferred_element_type=F32)


def roll_left(value, by):
    width = value.shape[1]
    by = by % width
    return value if by == 0 else pltpu.roll(value, width - by, 1)


def kernel(
    in_ref,
    cot_ref,
    gain_ref,
    wqkv_hbm,
    wproj_hbm,
    table_hbm,
    type_ref,
    region_ref,
    *rest,
):
    const_hbm = rest[:11]
    out_ref, gin_ref, ggain_ref, gqkv_ref, gproj_ref, gbias_ref = rest[11:17]
    wqkv, wproj, table = rest[17:20]
    const = rest[20:31]
    (
        slabs, qs, qr, rs, rr, keys, trow, amat, bias, gsb, gj, att,
        hs_own, hs_out, hs_in, as_own, as_out, as_in, gj_in, cw, cw_in,
        ysend, yrecv, xsend, xrecv, lsend, lrecv, bsend, brecv, asend, arecv,
        load_sem, halo_s, halo_r, back_s, back_r, sib_s, sib_r, y_s, y_r, x_s, x_r,
        l_s, l_r, b_s, b_r, a_s, a_r,
    ) = rest[31:]
    pack, pack_t, order, order_t, toep, dup, dup_t, key_rows, key_cols, key_cols_t, halves = const

    i = lax.axis_index("lat")
    j = lax.axis_index("lon")
    y, x, core = i // 4, (i // 2) % 2, i % 2
    sibling = (i + 1 - 2 * core, j)
    up, down = (i + 15) % 16, (i + 1) % 16
    left, right = (j + 15) % 16, (j + 1) % 16

    def remote(src, dst, ssem, rsem, dev):
        return pltpu.make_async_remote_copy(
            src_ref=src, dst_ref=dst, send_sem=ssem, recv_sem=rsem,
            device_id=dev, device_id_type=MESH,
        )

    loads = [
        pltpu.make_async_copy(s, d, load_sem.at[n])
        for n, (s, d) in enumerate(
            zip(
                (*const_hbm, wqkv_hbm, wproj_hbm, table_hbm),
                (*const, wqkv, wproj, table),
            )
        )
    ]
    for c in loads:
        c.start()

    barrier = pltpu.get_barrier_semaphore()

    def greet(d, carry):
        pl.semaphore_signal(barrier, inc=1, device_id=((i + d) % 16, j), device_id_type=MESH)
        pl.semaphore_signal(barrier, inc=1, device_id=(i, (j + d) % 16), device_id_type=MESH)
        return carry

    lax.fori_loop(1, 16, greet, 0)
    pl.semaphore_signal(barrier, inc=1, device_id=(up, left), device_id_type=MESH)
    pl.semaphore_signal(barrier, inc=1, device_id=(down, right), device_id_type=MESH)

    slabs[...] = jnp.zeros((384, 384), BF16)
    for l in range(2):
        for r in range(6):
            s = 16 * (6 * l + r)
            slabs[s : s + 12, :] = in_ref[l, r]
            slabs[192 + s : 192 + s + 12, :] = cot_ref[l, r]
    loads[0].wait()
    packed = dot(pack[...], slabs[...]).astype(BF16)
    for k in range(4):
        qs[k] = packed[80 * k : 80 * k + 80]
    pl.semaphore_wait(barrier, 32)
    halo = [
        remote(qs.at[k], qr.at[k], halo_s.at[k], halo_r.at[k], dev)
        for k, dev in enumerate(((up, left), (up, j), (i, left)))
    ]
    for c in halo:
        c.start()

    for n in range(1, 11):
        loads[n].wait()
    row_id = lax.broadcasted_iota(jnp.int32, (6, 12), 0)
    lat_side = (6 * i + row_id + 3 >= 96).astype(jnp.int32) * 2
    keys[...] = jnp.zeros((16, 128), F32)
    keys[0:6, 0:12] = (region_ref[0] * 4 + lat_side).astype(F32)
    keys[8:14, 0:12] = (region_ref[1] * 4 + lat_side + 1).astype(F32)
    key_grid = keys[...].astype(BF16)
    key_p = jnp.sum(
        dot(key_rows[...], key_grid) * key_cols[...].astype(F32), 1, keepdims=True
    )
    key_q = jnp.sum(
        dot(key_grid, key_rows[...], 0, 1) * key_cols_t[...].astype(F32), 0, keepdims=True
    )
    allowed = key_p == key_q

    loads[13].wait()
    kind = type_ref[0, 0]
    trow[...] = jnp.zeros((16, 3456), F32)
    trow[0:12, 0:3312] = table[kind].astype(F32)
    for zp in range(2):
        for ip in range(6):
            for b in range(4):
                off = ((2 * zp + b // 2) * 36 + 6 * ip + 3 * (b % 2)) * 23
                a = off // 128 * 128
                piece = roll_left(trow[:, a : a + 256], off - a)[:, :128]
                row = (6 * zp + ip) * 16
                amat[row : row + 16, 128 * b : 128 * b + 128] = piece.astype(BF16)
    spread0 = dot(dup[0], amat[...]).astype(BF16)
    spread1 = dot(dup[1], amat[...]).astype(BF16)
    for m in range(6):
        part = dot(spread0, toep[m, 0:512]) + dot(spread1, toep[m, 512:1024])
        ok = allowed[24 * m : 24 * m + 24]
        for h in range(12):
            bias[h, 24 * m : 24 * m + 24, :] = jnp.where(ok, part[24 * h : 24 * h + 24], -1e30)
    loads[11].wait()
    loads[12].wait()

    for c in halo:
        c.wait_recv()
    tokens = jnp.concatenate([qr[0], qr[1], qr[2], qs[3]], 0)
    both = dot(order[...], tokens)
    wide = both[0:144]
    cw[...] = both[144:288].astype(BF16)
    to_sib = [
        remote(cw, cw_in, sib_s.at[0], sib_r.at[0], sibling),
        remote(hs_out, hs_in, sib_s.at[1], sib_r.at[1], sibling),
        remote(as_out, as_in, sib_s.at[2], sib_r.at[2], sibling),
        remote(gj, gj_in, sib_s.at[3], sib_r.at[3], sibling),
    ]
    to_sib[0].start()

    def split_halves(value, own, out):
        spread = dot(value, halves[...]).astype(BF16)
        first, second = spread[:, 0:256], spread[:, 256:512]
        own[...] = jnp.where(core == 0, first, second)
        out[...] = jnp.where(core == 0, second, first)

    gain = gain_ref[...]
    center = jnp.mean(wide, 1, keepdims=True)
    shifted = wide - center
    inv_std = lax.rsqrt(jnp.mean(jnp.square(shifted), 1, keepdims=True) + 1e-05)
    normed = shifted * inv_std
    hidden = (normed * gain).astype(BF16)
    joined = dot(hidden, wqkv[...]).astype(BF16)
    split_halves(hidden, hs_own, hs_out)
    to_sib[1].start()
    cot_rows = cw[...]
    grad_att = dot(cot_rows, wproj[...], 1, 1).astype(BF16)

    lane_head = lax.broadcasted_iota(jnp.int32, (1, 128), 1) // 32
    head_masks = [(lane_head == h).astype(F32).astype(BF16) for h in range(4)]
    wide_masks = [(lane_head == h).astype(F32) for h in range(4)]

    def pick(stacked):
        total = stacked[0:144] * wide_masks[0]
        for h in range(1, 4):
            total = total + stacked[144 * h : 144 * h + 144] * wide_masks[h]
        return total

    for g in range(3):
        lanes = slice(128 * g, 128 * g + 128)
        queries = joined[:, 128 * g : 128 * g + 128]
        key_part = joined[:, 384 + 128 * g : 384 + 128 * g + 128]
        value_part = joined[:, 768 + 128 * g : 768 + 128 * g + 128]
        grad_part = grad_att[:, lanes]
        queries4 = jnp.concatenate([queries * k for k in head_masks], 0)
        grad4 = jnp.concatenate([grad_part * k for k in head_masks], 0)
        scores = dot(queries4, key_part, 1, 1) * SCALE
        scores = scores + bias[4 * g : 4 * g + 4].reshape(576, 144)
        top = jnp.max(scores, 1, keepdims=True)
        probs = jnp.exp(scores - top)
        probs = probs * (1.0 / jnp.sum(probs, 1, keepdims=True))
        probs_low = probs.astype(BF16)
        att[:, lanes] = pick(dot(probs_low, value_part)).astype(BF16)
        grad_probs = dot(grad4, value_part, 1, 1)
        grad_values = dot(probs_low, grad4, 0, 0)
        grad_scores = probs * (grad_probs - jnp.sum(probs * grad_probs, 1, keepdims=True))
        for h in range(4):
            for m in range(6):
                row = 24 * (4 * g + h)
                gsb[m, row : row + 24, :] = grad_scores[144 * h + 24 * m : 144 * h + 24 * m + 24]
        grad_scaled = (grad_scores * SCALE).astype(BF16)
        grad_query = pick(dot(grad_scaled, key_part))
        grad_keys = dot(grad_scaled, queries4, 0, 0)
        gj[:, 128 * g : 128 * g + 128] = grad_query.astype(BF16)
        gj[:, 384 + 128 * g : 384 + 128 * g + 128] = grad_keys.astype(BF16)
        gj[:, 768 + 128 * g : 768 + 128 * g + 128] = grad_values.astype(BF16)
    to_sib[3].start()
    attended = att[...]
    split_halves(attended, as_own, as_out)
    to_sib[2].start()

    result = (wide + dot(attended, wproj[...])).astype(BF16)
    grad_hidden = dot(gj[...], wqkv[...], 1, 1)
    grad_gain = jnp.sum(grad_hidden * normed, 0, keepdims=True)
    grad_normed = grad_hidden * gain
    grad_wide = inv_std * (
        grad_normed
        - jnp.mean(grad_normed, 1, keepdims=True)
        - normed * jnp.mean(grad_normed * normed, 1, keepdims=True)
    )
    grad_in = (cot_rows.astype(F32) + grad_wide).astype(BF16)
    returned = dot(order_t[...], jnp.concatenate([result, grad_in], 0)).astype(BF16)
    for k in range(4):
        rs[k] = returned[80 * k : 80 * k + 80]
    back = [
        remote(rs.at[k], rr.at[k], back_s.at[k], back_r.at[k], dev)
        for k, dev in enumerate(((down, right), (down, j), (i, right)))
    ]
    for c in back:
        c.start()

    folded = dot(gsb[0].astype(BF16), toep[0], 1, 1)
    for m in range(1, 6):
        folded = folded + dot(gsb[m].astype(BF16), toep[m], 1, 1)
    folded = folded.astype(BF16)
    shares = dot(dup_t[0], folded[:, 0:512]) + dot(dup_t[1], folded[:, 512:1024])
    block_row = lax.broadcasted_iota(jnp.int32, (16, 128), 0)

    def riders(gain_row, kind_row):
        high = gain_row.astype(BF16).astype(F32)
        low = gain_row - high
        return [
            jnp.where(block_row == 12, high[:, 128 * b : 128 * b + 128], 0.0)
            + jnp.where(block_row == 13, low[:, 128 * b : 128 * b + 128], 0.0)
            + jnp.where(block_row == 14, kind_row, 0.0)
            for b in range(3)
        ]

    extra = riders(grad_gain, kind.astype(F32))
    for dest in range(16):
        zp, zq, k = dest // 8, (dest // 4) % 2, dest % 4
        for b in range(3):
            ip, iqh = (3 * k + b) // 2, (3 * k + b) % 2
            row, lane = (6 * zp + ip) * 16, (2 * zq + iqh) * 128
            block = shares[row : row + 16, lane : lane + 128] + extra[b]
            bsend[dest, :, 128 * b : 128 * b + 128] = block.astype(BF16)

    def bias_lon(d):
        to = (j + d) % 16
        return remote(bsend.at[to], brecv.at[d], b_s.at[d], b_r.at[d], (i, to))

    def start_all(make):
        def body(d, carry):
            make(d).start()
            return carry

        lax.fori_loop(1, 16, body, 0)

    def wait_all(make):
        def body(d, carry):
            make(d).wait_recv()
            return carry

        lax.fori_loop(1, 16, body, 0)

    def sent_all(make):
        def body(d, carry):
            make(d).wait_send()
            return carry

        lax.fori_loop(1, 16, body, 0)

    start_all(bias_lon)

    for c in to_sib:
        c.wait_recv()
    g_qkv = dot(hs_own[...], gj[...], 0, 0) + dot(hs_in[...], gj_in[...], 0, 0)
    g_proj = dot(as_own[...], cw[...], 0, 0) + dot(as_in[...], cw_in[...], 0, 0)
    for k in range(4):
        ysend[k, :, 0:1152] = g_qkv[48 * k : 48 * k + 48].astype(BF16)
        ysend[k, :, 1152:1536] = g_proj[48 * k : 48 * k + 48].astype(BF16)

    def to_y(d):
        k = (y + d) % 4
        return remote(
            ysend.at[k], yrecv.at[d], y_s.at[d], y_r.at[d], (4 * k + 2 * x + core, j)
        )

    y_copies = [to_y(d) for d in range(1, 4)]
    for c in y_copies:
        c.start()

    wait_all(bias_lon)
    total = bsend[j].astype(F32)
    for d in range(1, 16):
        total = total + brecv[d].astype(F32)
    gain_lon = total[12:13] + total[13:14]
    kinds = total[14:15, 0:1] * (1.0 / 16.0)
    extra = riders(gain_lon, kinds)
    for b in range(3):
        lanes = slice(128 * b, 128 * b + 128)
        block = jnp.where(block_row < 12, total[:, lanes], 0.0) + extra[b]
        asend[:, lanes] = block.astype(BF16)

    def bias_lat(d):
        return remote(asend, arecv.at[d], a_s.at[d], a_r.at[d], ((i + d) % 16, j))

    start_all(bias_lat)

    for c in back:
        c.wait_recv()
    tokens = jnp.concatenate([rr[0], rr[1], rr[2], rs[3]], 0)
    final = dot(pack_t[...], tokens).astype(BF16)
    for l in range(2):
        for r in range(6):
            s = 16 * (6 * l + r)
            out_ref[l, r] = final[s : s + 12]
            gin_ref[l, r] = final[192 + s : 192 + s + 12]

    for c in y_copies:
        c.wait_recv()
    chunk = ysend[y].astype(F32)
    for d in range(1, 4):
        chunk = chunk + yrecv[d].astype(F32)
    mine = jnp.where(x == 0, chunk[0:24], chunk[24:48])
    other = jnp.where(x == 0, chunk[24:48], chunk[0:24])
    xsend[...] = jnp.concatenate([other[:, 0:768], other[:, 768:1536]], 0).astype(BF16)
    to_x = remote(xsend, xrecv, x_s, x_r, (4 * y + 2 * (1 - x) + core, j))
    to_x.start()

    wait_all(bias_lat)
    gain_total = jnp.zeros((1, 384), F32)
    sums = [jnp.zeros((16, 384), F32), jnp.zeros((16, 384), F32)]
    for d in range(16):
        block = asend[...] if d == 0 else arecv[d]
        block = block.astype(F32)
        gain_total = gain_total + block[12:13] + block[13:14]
        kind_row = block[14:15]
        for t in range(2):
            hit = kind_row == (2 * i + t).astype(F32)
            sums[t] = sums[t] + jnp.where(hit, block, 0.0)
    ggain_ref[...] = gain_total
    lane256 = lax.broadcasted_iota(jnp.int32, (16, 256), 1)
    for t in range(2):
        parts = [
            pltpu.roll(
                jnp.concatenate(
                    [sums[t][:, 128 * b : 128 * b + 128], jnp.zeros((16, 128), F32)], 1
                ),
                69 * b,
                1,
            )
            if b
            else jnp.concatenate([sums[t][:, 0:128], jnp.zeros((16, 128), F32)], 1)
            for b in range(3)
        ]
        row = jnp.where(lane256 < 69, parts[0], jnp.where(lane256 < 138, parts[1], parts[2]))
        gbias_ref[t] = row[0:12, 0:207]

    to_x.wait_recv()
    got = xrecv[...].astype(F32)
    mine = mine + jnp.concatenate([got[0:24], got[24:48]], 1)
    lane128 = lax.broadcasted_iota(jnp.int32, (24, 128), 1)
    for dest in range(16):
        off = 72 * dest
        a = min(off // 128 * 128, 896)
        piece = roll_left(mine[:, a : a + 256], off - a)[:, :128]
        off = 24 * dest
        a = min(off // 128 * 128, 128)
        tail = roll_left(mine[:, 1152 + a : 1152 + a + 256], off - a - 72)[:, :128]
        block = jnp.where(lane128 < 72, piece, tail)
        block = jnp.concatenate([block, jnp.zeros((8, 128), F32)], 0)
        lsend[dest] = block.astype(BF16)

    def to_lon(d):
        to = (j + d) % 16
        return remote(lsend.at[to], lrecv.at[d], l_s.at[d], l_r.at[d], (i, to))

    start_all(to_lon)
    for c in (*halo, *to_sib, *back, *y_copies, to_x):
        c.wait_send()
    sent_all(bias_lon)
    sent_all(bias_lat)
    wait_all(to_lon)
    total = lsend[j].astype(F32)
    for d in range(1, 16):
        total = total + lrecv[d].astype(F32)
    gqkv_ref[...] = total[0:24, 0:72]
    gproj_ref[...] = roll_left(total[0:24], 72)[:, 0:24]
    sent_all(to_lon)


def local(inputs, cotangent, norm_gain, qkv_weight, proj_weight, bias_table, window_type, region):
    consts = patterns()
    vmem = pl.BlockSpec(memory_space=pltpu.VMEM)
    anywhere = pl.BlockSpec(memory_space=pl.ANY)
    dma = pltpu.SemaphoreType.DMA
    tokens = (2, 6, 12, 384)
    outs = pl.pallas_call(
        kernel,
        out_shape=[
            jax.ShapeDtypeStruct(tokens, BF16),
            jax.ShapeDtypeStruct(tokens, BF16),
            jax.ShapeDtypeStruct((1, 384), F32),
            jax.ShapeDtypeStruct((24, 72), F32),
            jax.ShapeDtypeStruct((24, 24), F32),
            jax.ShapeDtypeStruct((2, 12, 207), F32),
        ],
        in_specs=[vmem, vmem, vmem, anywhere, anywhere, anywhere]
        + [pl.BlockSpec(memory_space=pltpu.SMEM), vmem]
        + [anywhere] * len(consts),
        out_specs=[vmem] * 6,
        scratch_shapes=[
            pltpu.VMEM(qkv_weight.shape, BF16),
            pltpu.VMEM(proj_weight.shape, BF16),
            pltpu.VMEM(bias_table.shape, BF16),
        ]
        + [pltpu.VMEM(c.shape, BF16) for c in consts]
        + [
            pltpu.VMEM((384, 384), BF16),
            pltpu.VMEM((4, 80, 384), BF16),
            pltpu.VMEM((3, 80, 384), BF16),
            pltpu.VMEM((4, 80, 384), BF16),
            pltpu.VMEM((3, 80, 384), BF16),
            pltpu.VMEM((16, 128), F32),
            pltpu.VMEM((16, 3456), F32),
            pltpu.VMEM((192, 512), BF16),
            pltpu.VMEM((12, 144, 144), F32),
            pltpu.VMEM((6, 288, 144), F32),
            pltpu.VMEM((144, 1152), BF16),
            pltpu.VMEM((144, 384), BF16),
            pltpu.VMEM((144, 256), BF16),
            pltpu.VMEM((144, 256), BF16),
            pltpu.VMEM((144, 256), BF16),
            pltpu.VMEM((144, 256), BF16),
            pltpu.VMEM((144, 256), BF16),
            pltpu.VMEM((144, 256), BF16),
            pltpu.VMEM((144, 1152), BF16),
            pltpu.VMEM((144, 384), BF16),
            pltpu.VMEM((144, 384), BF16),
            pltpu.VMEM((4, 48, 1536), BF16),
            pltpu.VMEM((4, 48, 1536), BF16),
            pltpu.VMEM((48, 768), BF16),
            pltpu.VMEM((48, 768), BF16),
            pltpu.VMEM((16, 32, 128), BF16),
            pltpu.VMEM((16, 32, 128), BF16),
            pltpu.VMEM((16, 16, 384), BF16),
            pltpu.VMEM((16, 16, 384), BF16),
            pltpu.VMEM((16, 384), BF16),
            pltpu.VMEM((16, 16, 384), BF16),
            dma((len(consts) + 3,)),
            dma((3,)), dma((3,)), dma((3,)), dma((3,)), dma((4,)), dma((4,)),
            dma((4,)), dma((4,)), dma, dma,
            dma((16,)), dma((16,)), dma((16,)), dma((16,)), dma((16,)), dma((16,)),
        ],
        compiler_params=pltpu.CompilerParams(
            collective_id=0, has_side_effects=True, vmem_limit_bytes=48 * 2**20
        ),
    )(
        inputs,
        cotangent,
        norm_gain.reshape(1, -1),
        qkv_weight,
        proj_weight,
        bias_table,
        window_type,
        region,
        *consts,
    )
    block_out, grad_inputs, grad_gain, grad_qkv, grad_proj, grad_bias = outs
    return block_out, grad_inputs, grad_gain.reshape(-1), grad_qkv, grad_proj, grad_bias


def solution(mesh):
    return jax.shard_map(
        local,
        mesh=mesh,
        in_specs=(
            P(None, "lat", "lon", None),
            P(None, "lat", "lon", None),
            P(),
            P(),
            P(),
            P(),
            P("lat", None),
            P(None, "lat", "lon"),
        ),
        out_specs=(
            P(None, "lat", "lon", None),
            P(None, "lat", "lon", None),
            P(),
            P("lat", "lon"),
            P("lat", "lon"),
            P("lat", None, "lon"),
        ),
        check_vma=False,
    )
```

```python
import functools

import jax
import jax.numpy as jnp
import numpy as np
from jax import lax
from jax.experimental import pallas as pl
from jax.experimental.pallas import tpu as pltpu
from jax.sharding import PartitionSpec as P

F32 = jnp.float32
BF16 = jnp.bfloat16
MESH = pl.DeviceIdType.MESH
SCALE = 32 ** (-0.5)


def patterns():
    order = np.zeros((144, 144), np.float32)
    toeplitz = np.zeros((6, 1024, 144), np.float32)
    dup = np.zeros((2, 288, 192), np.float32)
    key_rows = np.zeros((144, 16), np.float32)
    key_cols = np.zeros((144, 128), np.float32)
    halves = np.zeros((384, 384), np.float32)
    for l in range(2):
        for r in range(6):
            for c in range(12):
                p = 12 * c + 6 * l + r
                order[p, 24 * r + 2 * c + l] = 1
                key_rows[p, 2 * ((r + 3) % 6) + 1 - l] = 1
                key_cols[p, (c + 6) % 12] = 1
                for m in range(6):
                    for par in range(2):
                        spot = (2 * m + par + 6) % 12 - (c + 6) % 12 + 11
                        iq = (r + 3) % 6
                        lane = ((1 - l) * 2 + iq // 3) * 128 + (iq % 3) * 23 + spot
                        toeplitz[m, 512 * par + lane, p] = 1
    for h in range(12):
        for par in range(2):
            for l in range(2):
                for r in range(6):
                    zi = (1 - l) * 6 + (r + 3) % 6
                    dup[par, 24 * h + 12 * par + 6 * l + r, 16 * zi + h] = 1
    for f in range(384):
        i = f // 24
        halves[192 * (i % 2) + 24 * (i // 2) + f % 24, f] = 1
    both = [
        order,
        order.T,
        toeplitz,
        dup,
        dup.transpose(0, 2, 1),
        key_rows,
        key_cols,
        key_cols.T,
        halves,
    ]
    return [jnp.asarray(x, BF16) for x in both]


def dot(a, b, ca=1, cb=0):
    return lax.dot_general(a, b, (((ca,), (cb,)), ((), ())), preferred_element_type=F32)


def roll_left(value, by):
    width = value.shape[1]
    by = by % width
    return value if by == 0 else pltpu.roll(value, width - by, 1)


def kernel(
    in_hbm,
    cot_hbm,
    gain_hbm,
    wqkv_hbm,
    wproj_hbm,
    table_hbm,
    region_hbm,
    type_ref,
    *rest,
):
    const_hbm = rest[:9]
    out_ref, gin_ref, ggain_ref, gqkv_ref, gproj_ref, gbias_ref = rest[9:15]
    gain_ref, wqkv, wproj, table, region_ref = rest[15:20]
    const = rest[20:29]
    (
        win, win_cot, res, res_cot, tok, keys, trow, amat, bias, probs, gsb, gj, att,
        hs_own, hs_out, hs_in, as_own, as_out, as_in, gj_in, cw, cw_in,
        ysend, yrecv, xsend, xrecv, lsend, lrecv, bsend, brecv, asend, arecv,
        load_sem, own_sem, halo_s, halo_r, back_s, back_r, sib_s, sib_r, y_s, y_r, x_s, x_r,
        l_s, l_r, b_s, b_r, a_s, a_r,
    ) = rest[29:]
    order, order_t, toep, dup, dup_t, key_rows, key_cols, key_cols_t, halves = const

    i = lax.axis_index("lat")
    j = lax.axis_index("lon")
    y, x, core = i // 4, (i // 2) % 2, i % 2
    sibling = (i + 1 - 2 * core, j)
    up, down = (i + 15) % 16, (i + 1) % 16
    left, right = (j + 15) % 16, (j + 1) % 16

    def remote(src, dst, ssem, rsem, dev):
        return pltpu.make_async_remote_copy(
            src_ref=src, dst_ref=dst, send_sem=ssem, recv_sem=rsem,
            device_id=dev, device_id_type=MESH,
        )

    barrier = pltpu.get_barrier_semaphore()

    def greet(d, carry):
        pl.semaphore_signal(barrier, inc=1, device_id=((i + d) % 16, j), device_id_type=MESH)
        pl.semaphore_signal(barrier, inc=1, device_id=(i, (j + d) % 16), device_id_type=MESH)
        return carry

    pl.semaphore_signal(barrier, inc=1, device_id=(up, left), device_id_type=MESH)
    pl.semaphore_signal(barrier, inc=1, device_id=(down, right), device_id_type=MESH)
    lax.fori_loop(1, 16, greet, 0)

    own = [
        pltpu.make_async_copy(s.at[3:6, 6:12], d.at[3:6, 6:12], own_sem.at[n])
        for n, (s, d) in enumerate(((in_hbm, win), (cot_hbm, win_cot)))
    ]
    loads = [
        pltpu.make_async_copy(s, d, load_sem.at[n])
        for n, (s, d) in enumerate(
            zip(
                (table_hbm, region_hbm, gain_hbm, wqkv_hbm, wproj_hbm, *const_hbm),
                (table, region_ref, gain_ref, wqkv, wproj, *const),
            )
        )
    ]
    for c in (*own, *loads):
        c.start()

    corners = (
        ((slice(0, 3), slice(0, 6)), (up, left), (down, right)),
        ((slice(0, 3), slice(6, 12)), (up, j), (down, j)),
        ((slice(3, 6), slice(0, 6)), (i, left), (i, right)),
    )
    halo = [
        remote(s.at[spot], d.at[spot], halo_s.at[3 * n + k], halo_r.at[3 * n + k], dev)
        for n, (s, d) in enumerate(((in_hbm, win), (cot_hbm, win_cot)))
        for k, (spot, dev, _) in enumerate(corners)
    ]
    pl.semaphore_wait(barrier, 32)
    for c in halo:
        c.start()

    for c in loads:
        c.wait()
    for n in range(6):
        lat_side = (6 * i + n + 3 >= 96).astype(jnp.int32) * 2
        level = lax.broadcasted_iota(jnp.int32, (2, 12), 0)
        keys[2 * n : 2 * n + 2, 0:12] = (region_ref[n] * 4 + lat_side + level).astype(F32)
    in_grid = (lax.broadcasted_iota(jnp.int32, (16, 128), 0) < 12) & (
        lax.broadcasted_iota(jnp.int32, (16, 128), 1) < 12
    )
    key_grid = jnp.where(in_grid, keys[...], 0.0).astype(BF16)
    key_p = jnp.sum(
        dot(key_rows[...], key_grid) * key_cols[...].astype(F32), 1, keepdims=True
    )
    key_q = jnp.sum(
        dot(key_grid, key_rows[...], 0, 1) * key_cols_t[...].astype(F32), 0, keepdims=True
    )
    allowed = key_p == key_q

    kind = type_ref[0, 0]
    trow[...] = jnp.zeros((16, 3456), F32)
    is_kind = lax.broadcasted_iota(jnp.int32, (32, 3312), 0) == kind
    for h in range(12):
        trow[h : h + 1, 0:3312] = jnp.sum(
            jnp.where(is_kind, table[h].astype(F32), 0.0), 0, keepdims=True
        )
    for zp in range(2):
        for ip in range(6):
            for b in range(4):
                off = ((2 * zp + b // 2) * 36 + 6 * ip + 3 * (b % 2)) * 23
                a = off // 128 * 128
                piece = roll_left(trow[:, a : a + 256], off - a)[:, :128]
                row = (6 * zp + ip) * 16
                amat[row : row + 16, 128 * b : 128 * b + 128] = piece.astype(BF16)
    spread0 = dot(dup[0], amat[...]).astype(BF16)
    spread1 = dot(dup[1], amat[...]).astype(BF16)
    for m in range(6):
        part = dot(spread0, toep[m, 0:512]) + dot(spread1, toep[m, 512:1024])
        ok = allowed[24 * m : 24 * m + 24]
        for h in range(12):
            bias[h, 24 * m : 24 * m + 24, :] = jnp.where(ok, part[24 * h : 24 * h + 24], -1e30)

    def gather(source):
        for r in range(6):
            for c in range(12):
                k = 24 * r + 2 * c
                tok[k : k + 2, :] = source[r, c]
        return dot(order[...], tok[...])

    own[0].wait()
    for c in halo[0:3]:
        c.wait_recv()
    wide = gather(win)
    to_sib = [
        remote(src, dst, sib_s.at[n], sib_r.at[n], sibling)
        for n, (src, dst) in enumerate(
            [(cw, cw_in), (hs_out, hs_in), (as_out, as_in)]
            + [(gj.at[g], gj_in.at[g]) for g in range(3)]
        )
    ]

    def split_halves(value, own_half, out_half):
        spread = dot(halves[...], value, 1, 1).astype(BF16)
        first, second = spread[0:192], spread[192:384]
        own_half[...] = jnp.where(core == 0, first, second)
        out_half[...] = jnp.where(core == 0, second, first)

    def weight_part(n, left_own, left_in, right_own, right_in):
        part = dot(left_own[...], right_own) + dot(left_in[...], right_in)
        for k in range(4):
            ysend[n, k] = part[48 * k : 48 * k + 48].astype(BF16)

        def to_y(d):
            k = (y + d) % 4
            spot = 4 * n + d
            return remote(
                ysend.at[n, k], yrecv.at[n, d], y_s.at[spot], y_r.at[spot],
                (4 * k + 2 * x + core, j),
            )

        parts = [to_y(d) for d in range(1, 4)]
        for c in parts:
            c.start()
        return parts

    def put_back(value, target, n):
        back_rows = dot(order_t[...], value).astype(BF16)
        for r in range(6):
            for c in range(12):
                k = 24 * r + 2 * c
                target[r, c] = back_rows[k : k + 2]
        final = (out_ref, gin_ref)[n]
        sends = [
            remote(
                target.at[spot], final.at[spot],
                back_s.at[3 * n + k], back_r.at[3 * n + k], dev,
            )
            for k, (spot, _, dev) in enumerate(corners)
        ]
        kept = pltpu.make_async_copy(
            target.at[3:6, 6:12], final.at[3:6, 6:12], own_sem.at[2 + n]
        )
        for c in (*sends, kept):
            c.start()
        return sends, kept

    gain = gain_ref[...].reshape(1, 384)
    center = jnp.mean(wide, 1, keepdims=True)
    shifted = wide - center
    inv_std = lax.rsqrt(jnp.mean(jnp.square(shifted), 1, keepdims=True) + 1e-05)
    normed = shifted * inv_std
    hidden = (normed * gain).astype(BF16)
    joined = dot(hidden, wqkv[...]).astype(BF16)
    split_halves(hidden, hs_own, hs_out)
    to_sib[1].start()
    own[1].wait()
    for c in halo[3:6]:
        c.wait_recv()
    cw[...] = gather(win_cot).astype(BF16)
    to_sib[0].start()
    cot_rows = cw[...]
    grad_att = dot(cot_rows, wproj[...], 1, 1).astype(BF16)

    lane_head = lax.broadcasted_iota(jnp.int32, (1, 128), 1) // 32
    head_masks = [(lane_head == h).astype(F32).astype(BF16) for h in range(4)]
    wide_masks = [(lane_head == h).astype(F32) for h in range(4)]

    def pick(stacked):
        total = stacked[0:144] * wide_masks[0]
        for h in range(1, 4):
            total = total + stacked[144 * h : 144 * h + 144] * wide_masks[h]
        return total

    for g in range(3):
        lanes = slice(128 * g, 128 * g + 128)
        queries4 = jnp.concatenate([joined[:, lanes] * k for k in head_masks], 0)
        key_part = joined[:, 384 + 128 * g : 384 + 128 * g + 128]
        value_part = joined[:, 768 + 128 * g : 768 + 128 * g + 128]
        scores = dot(queries4, key_part, 1, 1) * SCALE
        scores = scores + bias[4 * g : 4 * g + 4].reshape(576, 144)
        top = jnp.max(scores, 1, keepdims=True)
        weights = jnp.exp(scores - top)
        weights = weights * (1.0 / jnp.sum(weights, 1, keepdims=True))
        probs[g] = weights
        att[:, lanes] = pick(dot(weights.astype(BF16), value_part)).astype(BF16)
    attended = att[...]
    split_halves(attended, as_own, as_out)
    to_sib[2].start()
    result = (wide + dot(attended, wproj[...])).astype(BF16)
    back_out, keep_out = put_back(result, res, 0)

    y_copies = []
    for g in range(3):
        lanes = slice(128 * g, 128 * g + 128)
        queries4 = jnp.concatenate([joined[:, lanes] * k for k in head_masks], 0)
        key_part = joined[:, 384 + 128 * g : 384 + 128 * g + 128]
        value_part = joined[:, 768 + 128 * g : 768 + 128 * g + 128]
        grad4 = jnp.concatenate([grad_att[:, lanes] * k for k in head_masks], 0)
        weights = probs[g]
        grad_probs = dot(grad4, value_part, 1, 1)
        grad_values = dot(weights.astype(BF16), grad4, 0, 0)
        grad_scores = weights * (grad_probs - jnp.sum(weights * grad_probs, 1, keepdims=True))
        for h in range(4):
            for m in range(6):
                row = 24 * (4 * g + h)
                gsb[m, row : row + 24, :] = grad_scores[144 * h + 24 * m : 144 * h + 24 * m + 24]
        grad_scaled = (grad_scores * SCALE).astype(BF16)
        grad_query = pick(dot(grad_scaled, key_part))
        grad_keys = dot(grad_scaled, queries4, 0, 0)
        gj[g, :, 0:128] = grad_query.astype(BF16)
        gj[g, :, 128:256] = grad_keys.astype(BF16)
        gj[g, :, 256:384] = grad_values.astype(BF16)
        to_sib[3 + g].start()
        if g == 0:
            to_sib[0].wait_recv()
            to_sib[2].wait_recv()
            y_copies.append(weight_part(0, as_own, as_in, cw[...], cw_in[...]))
            to_sib[1].wait_recv()
        else:
            to_sib[2 + g].wait_recv()
            y_copies.append(weight_part(g, hs_own, hs_in, gj[g - 1], gj_in[g - 1]))

    grad_joined = jnp.concatenate(
        [gj[g, :, 128 * n : 128 * n + 128] for n in range(3) for g in range(3)], 1
    )
    grad_hidden = dot(grad_joined, wqkv[...], 1, 1)
    to_sib[5].wait_recv()
    y_copies.append(weight_part(3, hs_own, hs_in, gj[2], gj_in[2]))

    grad_gain = jnp.sum(grad_hidden * normed, 0, keepdims=True)
    grad_normed = grad_hidden * gain
    grad_wide = inv_std * (
        grad_normed
        - jnp.mean(grad_normed, 1, keepdims=True)
        - normed * jnp.mean(grad_normed * normed, 1, keepdims=True)
    )
    grad_in = (cot_rows.astype(F32) + grad_wide).astype(BF16)
    back_grad, keep_grad = put_back(grad_in, res_cot, 1)

    folded = dot(gsb[0].astype(BF16), toep[0], 1, 1)
    for m in range(1, 6):
        folded = folded + dot(gsb[m].astype(BF16), toep[m], 1, 1)
    folded = folded.astype(BF16)
    shares = dot(dup_t[0], folded[:, 0:512]) + dot(dup_t[1], folded[:, 512:1024])
    share_row = lax.broadcasted_iota(jnp.int32, (16, 256), 0)
    share_lane = lax.broadcasted_iota(jnp.int32, (16, 256), 1)
    empty = jnp.zeros((16, 128), F32)

    def riders(gain_row, kind_row):
        high = gain_row.astype(BF16).astype(F32)
        low = gain_row - high
        rows = [
            high[:, 0:256],
            jnp.concatenate([high[:, 256:384], jnp.zeros((1, 128), F32)], 1),
            low[:, 0:256],
            jnp.concatenate([low[:, 256:384], jnp.zeros((1, 128), F32)], 1),
        ]
        block = jnp.where((share_row == 15) & (share_lane >= 128), kind_row, 0.0)
        for n, row in enumerate(rows):
            block = block + jnp.where(share_row == 12 + n, row, 0.0)
        return block

    def gain_of(block):
        return jnp.concatenate(
            [block[12:13] + block[14:15], block[13:14, 0:128] + block[15:16, 0:128]], 1
        )

    extra = riders(grad_gain, kind.astype(F32))
    for dest in range(16):
        zp, zq, k = dest // 8, (dest // 4) % 2, dest % 4
        block = extra
        for b in range(3):
            ip, iqh = (3 * k + b) // 2, (3 * k + b) % 2
            row, lane = (6 * zp + ip) * 16, (2 * zq + iqh) * 128
            piece = jnp.concatenate([shares[row : row + 16, lane : lane + 128], empty], 1)
            block = block + (pltpu.roll(piece, 69 * b, 1) if b else piece)
        bsend[dest] = block.astype(BF16)

    def bias_lon(d):
        to = (j + d) % 16
        return remote(bsend.at[to], brecv.at[d], b_s.at[d], b_r.at[d], (i, to))

    def start_all(make):
        def body(d, carry):
            make(d).start()
            return carry

        lax.fori_loop(1, 16, body, 0)

    def wait_all(make):
        def body(d, carry):
            make(d).wait_recv()
            return carry

        lax.fori_loop(1, 16, body, 0)

    def sent_all(make):
        def body(d, carry):
            make(d).wait_send()
            return carry

        lax.fori_loop(1, 16, body, 0)

    start_all(bias_lon)

    mine, x_copies = [], []
    for half in range(2):
        others = []
        for n in (2 * half, 2 * half + 1):
            for c in y_copies[n]:
                c.wait_recv()
            chunk = ysend[n, y].astype(F32)
            for d in range(1, 4):
                chunk = chunk + yrecv[n, d].astype(F32)
            mine.append(jnp.where(x == 0, chunk[0:24], chunk[24:48]))
            others.append(jnp.where(x == 0, chunk[24:48], chunk[0:24]))
        xsend[half] = jnp.concatenate(others, 0).astype(BF16)
        to_x = remote(
            xsend.at[half], xrecv.at[half], x_s.at[half], x_r.at[half],
            (4 * y + 2 * (1 - x) + core, j),
        )
        to_x.start()
        x_copies.append(to_x)

    wait_all(bias_lon)
    total = bsend[j].astype(F32)
    for d in range(1, 16):
        total = total + brecv[d].astype(F32)
    kinds = total[15:16, 128:129] * (1.0 / 16.0)
    block = jnp.where(share_row < 12, total, 0.0) + riders(gain_of(total), kinds)
    asend[...] = block.astype(BF16)

    def bias_lat(d):
        return remote(asend, arecv.at[d], a_s.at[d], a_r.at[d], ((i + d) % 16, j))

    start_all(bias_lat)

    for half, c in enumerate(x_copies):
        c.wait_recv()
        got = xrecv[half].astype(F32)
        mine[2 * half] = mine[2 * half] + got[0:24]
        mine[2 * half + 1] = mine[2 * half + 1] + got[24:48]
    own_qkv = jnp.concatenate(
        [mine[1 + g][:, 128 * n : 128 * n + 128] for n in range(3) for g in range(3)], 1
    )
    own_proj = mine[0]
    lane128 = lax.broadcasted_iota(jnp.int32, (24, 128), 1)
    for dest in range(16):
        off = 72 * dest
        a = min(off // 128 * 128, 896)
        piece = roll_left(own_qkv[:, a : a + 256], off - a)[:, :128]
        off = 24 * dest
        a = min(off // 128 * 128, 128)
        tail = roll_left(own_proj[:, a : a + 256], off - a - 72)[:, :128]
        block = jnp.where(lane128 < 72, piece, tail)
        block = jnp.concatenate([block, jnp.zeros((8, 128), F32)], 0)
        lsend[dest] = block.astype(BF16)

    def to_lon(d):
        to = (j + d) % 16
        return remote(lsend.at[to], lrecv.at[d], l_s.at[d], l_r.at[d], (i, to))

    start_all(to_lon)
    for c in (*halo, *to_sib, *back_out, *back_grad, *x_copies):
        c.wait_send()
    for parts in y_copies:
        for c in parts:
            c.wait_send()
    keep_out.wait()
    keep_grad.wait()
    sent_all(bias_lon)

    wait_all(bias_lat)
    gain_total = jnp.zeros((1, 384), F32)
    sums = [jnp.zeros((16, 256), F32), jnp.zeros((16, 256), F32)]
    for d in range(16):
        block = asend[...] if d == 0 else arecv[d]
        block = block.astype(F32)
        gain_total = gain_total + gain_of(block)
        for t in range(2):
            hit = block[15:16, 128:129] == (2 * i + t).astype(F32)
            sums[t] = sums[t] + jnp.where(hit, block, 0.0)
    ggain_ref[...] = gain_total.reshape(384)
    for h in range(12):
        row = jnp.concatenate([sums[0][h : h + 1, 0:207], sums[1][h : h + 1, 0:207]], 0)
        gbias_ref[h] = row
    sent_all(bias_lat)
    for c in (*back_out, *back_grad):
        c.wait_recv()

    wait_all(to_lon)
    total = lsend[j].astype(F32)
    for d in range(1, 16):
        total = total + lrecv[d].astype(F32)
    gqkv_ref[...] = total[0:24, 0:72]
    gproj_ref[...] = roll_left(total[0:24], 72)[:, 0:24]
    sent_all(to_lon)


def finish(*refs):
    for source, target in zip(refs[:6], refs[6:]):
        target[...] = source[...]


def local(inputs, cotangent, norm_gain, qkv_weight, proj_weight, bias_table, window_type, region):
    consts = patterns()
    vmem = pl.BlockSpec(memory_space=pltpu.VMEM)
    hbm = pl.BlockSpec(memory_space=pltpu.HBM)
    dma = pltpu.SemaphoreType.DMA
    tokens = (6, 12, 2, 384)
    shapes = [
        jax.ShapeDtypeStruct(tokens, BF16),
        jax.ShapeDtypeStruct(tokens, BF16),
        jax.ShapeDtypeStruct((384,), F32),
        jax.ShapeDtypeStruct((24, 72), F32),
        jax.ShapeDtypeStruct((24, 24), F32),
        jax.ShapeDtypeStruct((12, 2, 207), F32),
    ]
    outs = pl.pallas_call(
        kernel,
        out_shape=shapes,
        in_specs=[hbm] * 7 + [pl.BlockSpec(memory_space=pltpu.SMEM)] + [hbm] * len(consts),
        out_specs=[vmem] * 6,
        scratch_shapes=[
            pltpu.VMEM((384,), F32),
            pltpu.VMEM(qkv_weight.shape, BF16),
            pltpu.VMEM(proj_weight.shape, BF16),
            pltpu.VMEM((12, 32, 3312), BF16),
            pltpu.VMEM((6, 2, 12), jnp.int32),
        ]
        + [pltpu.VMEM(c.shape, BF16) for c in consts]
        + [
            pltpu.VMEM(tokens, BF16),
            pltpu.VMEM(tokens, BF16),
            pltpu.VMEM(tokens, BF16),
            pltpu.VMEM(tokens, BF16),
            pltpu.VMEM((144, 384), BF16),
            pltpu.VMEM((16, 128), F32),
            pltpu.VMEM((16, 3456), F32),
            pltpu.VMEM((192, 512), BF16),
            pltpu.VMEM((12, 144, 144), F32),
            pltpu.VMEM((3, 576, 144), F32),
            pltpu.VMEM((6, 288, 144), F32),
            pltpu.VMEM((3, 144, 384), BF16),
            pltpu.VMEM((144, 384), BF16),
            pltpu.VMEM((192, 144), BF16),
            pltpu.VMEM((192, 144), BF16),
            pltpu.VMEM((192, 144), BF16),
            pltpu.VMEM((192, 144), BF16),
            pltpu.VMEM((192, 144), BF16),
            pltpu.VMEM((192, 144), BF16),
            pltpu.VMEM((3, 144, 384), BF16),
            pltpu.VMEM((144, 384), BF16),
            pltpu.VMEM((144, 384), BF16),
            pltpu.VMEM((4, 4, 48, 384), BF16),
            pltpu.VMEM((4, 4, 48, 384), BF16),
            pltpu.VMEM((2, 48, 384), BF16),
            pltpu.VMEM((2, 48, 384), BF16),
            pltpu.VMEM((16, 32, 128), BF16),
            pltpu.VMEM((16, 32, 128), BF16),
            pltpu.VMEM((16, 16, 256), BF16),
            pltpu.VMEM((16, 16, 256), BF16),
            pltpu.VMEM((16, 256), BF16),
            pltpu.VMEM((16, 16, 256), BF16),
            dma((len(consts) + 5,)), dma((4,)),
            dma((6,)), dma((6,)), dma((6,)), dma((6,)), dma((6,)), dma((6,)),
            dma((16,)), dma((16,)), dma((2,)), dma((2,)),
            dma((16,)), dma((16,)), dma((16,)), dma((16,)), dma((16,)), dma((16,)),
        ],
        compiler_params=pltpu.CompilerParams(
            collective_id=0, has_side_effects=True, vmem_limit_bytes=62 * 2**20
        ),
    )(
        inputs.transpose(1, 2, 0, 3),
        cotangent.transpose(1, 2, 0, 3),
        norm_gain,
        qkv_weight,
        proj_weight,
        bias_table.transpose(1, 0, 2),
        region.transpose(1, 0, 2),
        window_type,
        *consts,
    )
    outs = pl.pallas_call(
        finish,
        out_shape=shapes,
        in_specs=[vmem] * 6,
        out_specs=[vmem] * 6,
    )(*outs)
    block_out, grad_inputs, grad_gain, grad_qkv, grad_proj, grad_bias = outs
    return (
        block_out.transpose(2, 0, 1, 3),
        grad_inputs.transpose(2, 0, 1, 3),
        grad_gain,
        grad_qkv,
        grad_proj,
        grad_bias.transpose(1, 0, 2),
    )


def solution(mesh):
    return jax.shard_map(
        local,
        mesh=mesh,
        in_specs=(
            P(None, "lat", "lon", None),
            P(None, "lat", "lon", None),
            P(),
            P(),
            P(),
            P(),
            P("lat", None),
            P(None, "lat", "lon"),
        ),
        out_specs=(
            P(None, "lat", "lon", None),
            P(None, "lat", "lon", None),
            P(),
            P("lat", "lon"),
            P("lat", "lon"),
            P("lat", None, "lon"),
        ),
        check_vma=False,
    )
```

```python
import functools

import jax
import jax.numpy as jnp
import numpy as np
from jax import lax
from jax.experimental import pallas as pl
from jax.experimental.pallas import tpu as pltpu
from jax.sharding import PartitionSpec as P

F32 = jnp.float32
BF16 = jnp.bfloat16
MESH = pl.DeviceIdType.MESH
SCALE = 32 ** (-0.5)


def patterns():
    order = np.zeros((144, 144), np.float32)
    toeplitz = np.zeros((6, 144, 768), np.float32)
    dup = np.zeros((2, 288, 192), np.float32)
    key_rows = np.zeros((144, 16), np.float32)
    key_cols = np.zeros((144, 128), np.float32)
    halves = np.zeros((384, 384), np.float32)
    for l in range(2):
        for r in range(6):
            for c in range(12):
                p = 12 * c + 6 * l + r
                order[p, 24 * r + 2 * c + l] = 1
                key_rows[p, 2 * ((r + 3) % 6) + 1 - l] = 1
                key_cols[p, (c + 6) % 12] = 1
                for m in range(6):
                    for par in range(2):
                        spot = (2 * m + par + 6) % 12 - (c + 6) % 12 + 11
                        iq = (r + 3) % 6
                        lane = (1 - l) * 138 + iq * 23 + spot
                        toeplitz[m, p, 384 * par + lane] = 1
    for h in range(12):
        for par in range(2):
            for l in range(2):
                for r in range(6):
                    zi = (1 - l) * 6 + (r + 3) % 6
                    dup[par, 24 * h + 12 * par + 6 * l + r, 16 * zi + h] = 1
    for f in range(384):
        i = f // 24
        halves[192 * (i % 2) + 24 * (i // 2) + f % 24, f] = 1
    both = [
        key_rows,
        key_cols,
        key_cols.T,
        dup,
        toeplitz,
        order,
        halves,
        order.T,
        dup.transpose(0, 2, 1),
    ]
    return [jnp.asarray(x, BF16) for x in both]


def dot(a, b, ca=1, cb=0):
    return lax.dot_general(a, b, (((ca,), (cb,)), ((), ())), preferred_element_type=F32)


def roll_left(value, by):
    width = value.shape[1]
    by = by % width
    return value if by == 0 else pltpu.roll(value, width - by, 1)


def kernel(
    in_hbm,
    cot_hbm,
    gain_hbm,
    wqkv_hbm,
    wproj_hbm,
    table_hbm,
    region_hbm,
    type_ref,
    *rest,
):
    const_hbm = rest[:9]
    out_ref, gin_ref, ggain_ref, gqkv_ref, gproj_ref, gbias_ref = rest[9:15]
    gain_ref, wqkv, wproj, table, region_ref = rest[15:20]
    const = rest[20:29]
    (
        win, win_cot, res, res_cot, out_own, gin_own, tok, keys, trow, amat, bias, probs, gsb, gqk, gv, att,
        hs_own, hs_out, hs_in, as_own, as_out, as_in, gqk_in, gv_in, cw, cw_in,
        ysend, yrecv, zsend, zrecv, xsend, xrecv, lsend, lrecv, bsend, brecv, asend, arecv,
        load_sem, own_sem, halo_s, halo_r, back_s, back_r, sib_s, sib_r, y_s, y_r, z_s, z_r, x_s, x_r,
        l_s, l_r, b_s, b_r, a_s, a_r,
    ) = rest[29:]
    key_rows, key_cols, key_cols_t, dup, toep, order, halves, order_t, dup_t = const

    i = lax.axis_index("lat")
    j = lax.axis_index("lon")
    y, x, core = i // 4, (i // 2) % 2, i % 2
    sibling = (i + 1 - 2 * core, j)
    up, down = (i + 15) % 16, (i + 1) % 16
    left, right = (j + 15) % 16, (j + 1) % 16

    def remote(src, dst, ssem, rsem, dev):
        return pltpu.make_async_remote_copy(
            src_ref=src, dst_ref=dst, send_sem=ssem, recv_sem=rsem,
            device_id=dev, device_id_type=MESH,
        )

    barrier = pltpu.get_barrier_semaphore()
    for dev in ((up, left), (down, right)):
        pl.semaphore_signal(barrier, inc=1, device_id=dev, device_id_type=MESH)

    def greet(d, carry):
        pl.semaphore_signal(barrier, inc=1, device_id=((i + d) % 16, j), device_id_type=MESH)
        pl.semaphore_signal(barrier, inc=1, device_id=(i, (j + d) % 16), device_id_type=MESH)
        return carry

    lax.fori_loop(1, 16, greet, 0)

    own = [
        pltpu.make_async_copy(s.at[3:6, 6:12], d.at[3:6, 6:12], own_sem.at[n])
        for n, (s, d) in enumerate(((in_hbm, win), (cot_hbm, win_cot)))
    ]
    loads = [
        pltpu.make_async_copy(s, d, load_sem.at[n])
        for n, (s, d) in enumerate(
            zip(
                (region_hbm, *const_hbm[:3], table_hbm, *const_hbm[3:6], gain_hbm, wqkv_hbm, const_hbm[6], wproj_hbm, *const_hbm[7:]),
                (region_ref, *const[:3], table, *const[3:6], gain_ref, wqkv, const[6], wproj, *const[7:]),
            )
        )
    ]
    for c in (*own, *loads):
        c.start()

    corners = (
        ((slice(0, 3), slice(0, 6)), (up, left), (down, right)),
        ((slice(0, 3), slice(6, 12)), (up, j), (down, j)),
        ((slice(3, 6), slice(0, 6)), (i, left), (i, right)),
    )
    halo = [
        remote(s.at[spot], d.at[spot], halo_s.at[3 * n + k], halo_r.at[3 * n + k], dev)
        for n, (s, d) in enumerate(((in_hbm, win), (cot_hbm, win_cot)))
        for k, (spot, dev, _) in enumerate(corners)
    ]
    pl.semaphore_wait(barrier, 32)
    for c in halo:
        c.start()

    for c in loads[0:4]:
        c.wait()
    for n in range(6):
        lat_side = (6 * i + n + 3 >= 96).astype(jnp.int32) * 2
        level = lax.broadcasted_iota(jnp.int32, (2, 12), 0)
        keys[2 * n : 2 * n + 2, 0:12] = (region_ref[n] * 4 + lat_side + level).astype(F32)
    in_grid = (lax.broadcasted_iota(jnp.int32, (16, 128), 0) < 12) & (
        lax.broadcasted_iota(jnp.int32, (16, 128), 1) < 12
    )
    key_grid = jnp.where(in_grid, keys[...], 0.0).astype(BF16)
    key_p = jnp.sum(
        dot(key_rows[...], key_grid) * key_cols[...].astype(F32), 1, keepdims=True
    )
    key_q = jnp.sum(
        dot(key_grid, key_rows[...], 0, 1) * key_cols_t[...].astype(F32), 0, keepdims=True
    )
    allowed = key_p == key_q

    kind = type_ref[0, 0]
    trow[...] = jnp.zeros((16, 3456), F32)
    is_kind = lax.broadcasted_iota(jnp.int32, (32, 3312), 0) == kind
    loads[4].wait()
    for h in range(12):
        trow[h : h + 1, 0:3312] = jnp.sum(
            jnp.where(is_kind, table[h].astype(F32), 0.0), 0, keepdims=True
        )
    wide_lane = lax.broadcasted_iota(jnp.int32, (16, 384), 1)
    for zp in range(2):
        for ip in range(6):
            pieces = []
            for zq in range(2):
                off = ((2 * zp + zq) * 36 + 6 * ip) * 23
                a = off // 128 * 128
                pieces.append(roll_left(trow[:, a : a + 384], off - a - 138 * zq))
            row = (6 * zp + ip) * 16
            amat[row : row + 16, :] = jnp.where(wide_lane < 138, *pieces).astype(BF16)
    loads[5].wait()
    spread = jnp.concatenate([dot(dup[0], amat[...]), dot(dup[1], amat[...])], 1).astype(BF16)
    loads[6].wait()
    for m in range(6):
        part = dot(spread, toep[m], 1, 1)
        ok = allowed[24 * m : 24 * m + 24]
        for h in range(12):
            bias[h, 24 * m : 24 * m + 24, :] = jnp.where(ok, part[24 * h : 24 * h + 24], -1e30)
    for c in loads[7:]:
        c.wait()

    def gather(source):
        for r in range(6):
            for c in range(12):
                k = 24 * r + 2 * c
                tok[k : k + 2, :] = source[r, c]
        return dot(order[...], tok[...])


    own[0].wait()
    for c in halo[0:3]:
        c.wait_recv()
    wide = gather(win)
    to_sib = [
        remote(src, dst, sib_s.at[n], sib_r.at[n], sibling)
        for n, (src, dst) in enumerate(
            [(cw, cw_in), (hs_out, hs_in), (as_out, as_in), (gv, gv_in)]
            + [(gqk.at[g], gqk_in.at[g]) for g in range(3)]
        )
    ]

    def split_halves(value, own_half, out_half):
        spread = dot(halves[...], value, 1, 1).astype(BF16)
        first, second = spread[0:192], spread[192:384]
        own_half[...] = jnp.where(core == 0, first, second)
        out_half[...] = jnp.where(core == 0, second, first)

    def whole(ref, ssem, rsem):
        return [pltpu.make_async_copy(ref, ref, sem) for sem in (ssem, rsem)]

    def weight_part(n, left_own, left_in, right_own, right_in):
        part = dot(left_own[...], right_own) + dot(left_in[...], right_in)
        if n >= 2:
            q = n - 2
            for k in range(8):
                rows = part[24 * k : 24 * k + 24]
                zsend[q, k] = jnp.concatenate([rows[:, 0:128], rows[:, 128:256]], 0).astype(BF16)

            def to_lat(d):
                k = 2 * ((y + d // 2) % 4) + (x + d) % 2
                return remote(
                    zsend.at[q, k], zrecv.at[q, d], z_s.at[q], z_r.at[q], (2 * k + core, j)
                )

            parts = [to_lat(d) for d in range(1, 8)]
            waits = whole(zrecv.at[q, pl.ds(1, 7)], z_s.at[q], z_r.at[q])
        else:
            for k in range(4):
                ysend[n, k] = part[48 * k : 48 * k + 48].astype(BF16)

            def to_y(d):
                k = (y + d) % 4
                return remote(
                    ysend.at[n, k], yrecv.at[n, d], y_s.at[n], y_r.at[n],
                    (4 * k + 2 * x + core, j),
                )

            parts = [to_y(d) for d in range(1, 4)]
            waits = whole(yrecv.at[n, pl.ds(1, 3)], y_s.at[n], y_r.at[n])
        for c in parts:
            c.start()
        return waits

    def over_x():
        keep, others = [], []
        for n in range(2):
            y_copies[n][1].wait()
            chunk = ysend[n, y].astype(F32)
            for d in range(1, 4):
                chunk = chunk + yrecv[n, d].astype(F32)
            keep.append(jnp.where(x == 0, chunk[0:24], chunk[24:48]))
            others.append(jnp.where(x == 0, chunk[24:48], chunk[0:24]))
        xsend[...] = jnp.concatenate(others, 0).astype(BF16)
        to_x = remote(xsend, xrecv, x_s, x_r, (4 * y + 2 * (1 - x) + core, j))
        to_x.start()
        return keep, to_x

    landed = (out_own, gin_own)

    def put_back(value, target, n):
        back_rows = dot(order_t[...], value).astype(BF16)
        for r in range(6):
            for c in range(12):
                k = 24 * r + 2 * c
                kept = r >= 3 and c >= 6
                (landed[n] if kept else target)[r, c] = back_rows[k : k + 2]
        sends = [
            remote(
                target.at[spot], landed[n].at[spot],
                back_s.at[3 * n + k], back_r.at[3 * n + k], dev,
            )
            for k, (spot, _, dev) in enumerate(corners)
        ]
        for c in sends:
            c.start()
        return sends

    gain = gain_ref[...].reshape(1, 384)
    center = jnp.mean(wide, 1, keepdims=True)
    shifted = wide - center
    inv_std = lax.rsqrt(jnp.mean(jnp.square(shifted), 1, keepdims=True) + 1e-05)
    normed = shifted * inv_std
    hidden = (normed * gain).astype(BF16)
    joined = dot(hidden, wqkv[...]).astype(BF16)
    split_halves(hidden, hs_own, hs_out)
    to_sib[1].start()
    own[1].wait()
    for c in halo[3:6]:
        c.wait_recv()
    cw[...] = gather(win_cot).astype(BF16)
    to_sib[0].start()
    cot_rows = cw[...]
    grad_att = dot(cot_rows, wproj[...], 1, 1).astype(BF16)

    lane_head = lax.broadcasted_iota(jnp.int32, (1, 128), 1) // 32
    head_masks = [(lane_head == h).astype(F32).astype(BF16) for h in range(4)]
    wide_masks = [(lane_head == h).astype(F32) for h in range(4)]

    def pick(stacked):
        total = stacked[0:144] * wide_masks[0]
        for h in range(1, 4):
            total = total + stacked[144 * h : 144 * h + 144] * wide_masks[h]
        return total

    for g in range(3):
        lanes = slice(128 * g, 128 * g + 128)
        queries4 = jnp.concatenate([joined[:, lanes] * k for k in head_masks], 0)
        key_part = joined[:, 384 + 128 * g : 384 + 128 * g + 128]
        value_part = joined[:, 768 + 128 * g : 768 + 128 * g + 128]
        scores = dot(queries4, key_part, 1, 1) * SCALE
        scores = scores + bias[4 * g : 4 * g + 4].reshape(576, 144)
        top = jnp.max(scores, 1, keepdims=True)
        weights = jnp.exp(scores - top)
        weights = weights * (1.0 / jnp.sum(weights, 1, keepdims=True))
        probs[g] = weights
        probs_low = weights.astype(BF16)
        att[:, lanes] = pick(dot(probs_low, value_part)).astype(BF16)
        grad4 = jnp.concatenate([grad_att[:, lanes] * k for k in head_masks], 0)
        gv[:, lanes] = dot(probs_low, grad4, 0, 0).astype(BF16)
    to_sib[3].start()
    attended = att[...]
    split_halves(attended, as_own, as_out)
    to_sib[2].start()

    result = (wide + dot(attended, wproj[...])).astype(BF16)
    back_out = put_back(result, res, 0)

    to_sib[1].wait_recv()
    to_sib[3].wait_recv()
    y_copies = [weight_part(0, hs_own, hs_in, gv[...], gv_in[...])]
    to_sib[0].wait_recv()
    to_sib[2].wait_recv()
    y_copies.append(weight_part(1, as_own, as_in, cw[...], cw_in[...]))
    for g in range(3):
        lanes = slice(128 * g, 128 * g + 128)
        queries4 = jnp.concatenate([joined[:, lanes] * k for k in head_masks], 0)
        key_part = joined[:, 384 + 128 * g : 384 + 128 * g + 128]
        value_part = joined[:, 768 + 128 * g : 768 + 128 * g + 128]
        grad4 = jnp.concatenate([grad_att[:, lanes] * k for k in head_masks], 0)
        weights = probs[g]
        grad_probs = dot(grad4, value_part, 1, 1)
        grad_scores = weights * (grad_probs - jnp.sum(weights * grad_probs, 1, keepdims=True))
        for h in range(4):
            for m in range(6):
                row = 24 * (4 * g + h)
                gsb[m, row : row + 24, :] = grad_scores[144 * h + 24 * m : 144 * h + 24 * m + 24]
        grad_scaled = (grad_scores * SCALE).astype(BF16)
        grad_query = pick(dot(grad_scaled, key_part))
        grad_keys = dot(grad_scaled, queries4, 0, 0)
        gqk[g, :, 0:128] = grad_query.astype(BF16)
        gqk[g, :, 128:256] = grad_keys.astype(BF16)
        to_sib[4 + g].start()
        if g > 0:
            to_sib[3 + g].wait_recv()
            y_copies.append(weight_part(1 + g, hs_own, hs_in, gqk[g - 1], gqk_in[g - 1]))

    grad_joined = jnp.concatenate(
        [gqk[g, :, 128 * n : 128 * n + 128] for n in range(2) for g in range(3)] + [gv[...]], 1
    )
    grad_hidden = dot(grad_joined, wqkv[...], 1, 1)
    grad_gain = jnp.sum(grad_hidden * normed, 0, keepdims=True)
    folded = dot(gsb[0].astype(BF16), toep[0])
    for m in range(1, 6):
        folded = folded + dot(gsb[m].astype(BF16), toep[m])
    folded = folded.astype(BF16)

    shares = dot(dup_t[0], folded[:, 0:384]) + dot(dup_t[1], folded[:, 384:768])
    share_row = lax.broadcasted_iota(jnp.int32, (16, 256), 0)
    share_lane = lax.broadcasted_iota(jnp.int32, (16, 256), 1)

    def riders(gain_row, kind_row):
        high = gain_row.astype(BF16).astype(F32)
        low = gain_row - high
        rows = [
            high[:, 0:256],
            jnp.concatenate([high[:, 256:384], jnp.zeros((1, 128), F32)], 1),
            low[:, 0:256],
            jnp.concatenate([low[:, 256:384], jnp.zeros((1, 128), F32)], 1),
        ]
        block = jnp.where((share_row == 15) & (share_lane >= 128), kind_row, 0.0)
        for n, row in enumerate(rows):
            block = block + jnp.where(share_row == 12 + n, row, 0.0)
        return block

    def gain_of(block):
        return jnp.concatenate(
            [block[12:13] + block[14:15], block[13:14, 0:128] + block[15:16, 0:128]], 1
        )

    extra = riders(grad_gain, kind.astype(F32))
    for dest in range(16):
        zp, zq, k = dest // 8, (dest // 4) % 2, dest % 4
        first = (6 * zp + 3 * k // 2) * 16
        edge = 69 if k % 2 else 138
        pieces = [
            roll_left(shares[row : row + 16], 138 * zq + start)[:, 0:256]
            for row, start in ((first, 138 - edge), (first + 16, -edge))
        ]
        block = jnp.where(share_lane < edge, *pieces)
        block = jnp.where((share_row < 12) & (share_lane < 207), block, 0.0) + extra
        bsend[dest] = block.astype(BF16)

    def bias_lon(d):
        to = (j + d) % 16
        return remote(bsend.at[to], brecv.at[d], b_s, b_r, (i, to))

    def start_all(make):
        def body(d, carry):
            make(d).start()
            return carry

        lax.fori_loop(1, 16, body, 0)

    all_lon = whole(lrecv.at[pl.ds(1, 15)], l_s, l_r)
    all_bias = whole(brecv.at[pl.ds(1, 15)], b_s, b_r)
    all_lat = whole(arecv.at[pl.ds(1, 15)], a_s, a_r)
    start_all(bias_lon)

    to_sib[6].wait_recv()
    y_copies.append(weight_part(4, hs_own, hs_in, gqk[2], gqk_in[2]))

    mine, to_x = over_x()
    grad_normed = grad_hidden * gain
    grad_wide = inv_std * (
        grad_normed
        - jnp.mean(grad_normed, 1, keepdims=True)
        - normed * jnp.mean(grad_normed * normed, 1, keepdims=True)
    )
    grad_in = (cot_rows.astype(F32) + grad_wide).astype(BF16)
    back_grad = put_back(grad_in, res_cot, 1)

    own_qk = []
    for q in range(3):
        y_copies[2 + q][1].wait()
        chunk = zsend[q, 2 * y + x].astype(F32)
        for d in range(1, 8):
            chunk = chunk + zrecv[q, d].astype(F32)
        own_qk.append(chunk)
    to_x.wait_recv()
    got = xrecv[...].astype(F32)
    own_value = mine[0] + got[0:24]
    own_proj = mine[1] + got[24:48]
    own_qkv = jnp.concatenate(
        [part[0:24] for part in own_qk] + [part[24:48] for part in own_qk] + [own_value],
        1,
    )
    lane128 = lax.broadcasted_iota(jnp.int32, (24, 128), 1)
    for dest in range(16):
        off = 72 * dest
        a = min(off // 128 * 128, 896)
        piece = roll_left(own_qkv[:, a : a + 256], off - a)[:, :128]
        off = 24 * dest
        a = min(off // 128 * 128, 128)
        tail = roll_left(own_proj[:, a : a + 256], off - a - 72)[:, :128]
        block = jnp.where(lane128 < 72, piece, tail)
        block = jnp.concatenate([block, jnp.zeros((8, 128), F32)], 0)
        lsend[dest] = block.astype(BF16)

    def to_lon(d):
        to = (j + d) % 16
        return remote(lsend.at[to], lrecv.at[d], l_s, l_r, (i, to))

    start_all(to_lon)

    all_bias[1].wait()
    total = bsend[j].astype(F32)
    for d in range(1, 16):
        total = total + brecv[d].astype(F32)
    kinds = total[15:16, 128:129] * (1.0 / 16.0)
    block = jnp.where(share_row < 12, total, 0.0) + riders(gain_of(total), kinds)
    asend[...] = block.astype(BF16)

    def bias_lat(d):
        return remote(asend, arecv.at[d], a_s, a_r, ((i + d) % 16, j))

    start_all(bias_lat)

    for c in (*halo, *to_sib, *back_out, *back_grad, to_x):
        c.wait_send()
    for sent, _ in y_copies:
        sent.wait()
    all_bias[0].wait()

    all_lat[1].wait()
    gain_total = jnp.zeros((1, 384), F32)
    sums = [jnp.zeros((16, 256), F32), jnp.zeros((16, 256), F32)]
    for d in range(16):
        block = asend[...] if d == 0 else arecv[d]
        block = block.astype(F32)
        gain_total = gain_total + gain_of(block)
        for t in range(2):
            hit = block[15:16, 128:129] == (2 * i + t).astype(F32)
            sums[t] = sums[t] + jnp.where(hit, block, 0.0)
    ggain_ref[...] = gain_total.reshape(384)
    for h in range(12):
        row = jnp.concatenate([sums[0][h : h + 1, 0:207], sums[1][h : h + 1, 0:207]], 0)
        gbias_ref[h] = row
    all_lat[0].wait()
    writes = []
    for n, (copies, target) in enumerate(((back_out, out_ref), (back_grad, gin_ref))):
        for c in copies:
            c.wait_recv()
        writes.append(pltpu.make_async_copy(landed[n], target, own_sem.at[2 + n]))
        writes[n].start()

    all_lon[1].wait()
    total = lsend[j].astype(F32)
    for d in range(1, 16):
        total = total + lrecv[d].astype(F32)
    gqkv_ref[...] = total[0:24, 0:72]
    gproj_ref[...] = roll_left(total[0:24], 72)[:, 0:24]
    all_lon[0].wait()
    for c in writes:
        c.wait()


def finish(*refs):
    for source, target in zip(refs[:6], refs[6:]):
        target[...] = source[...]


def local(inputs, cotangent, norm_gain, qkv_weight, proj_weight, bias_table, window_type, region):
    consts = patterns()
    vmem = pl.BlockSpec(memory_space=pltpu.VMEM)
    hbm = pl.BlockSpec(memory_space=pltpu.HBM)
    dma = pltpu.SemaphoreType.DMA
    tokens = (6, 12, 2, 384)
    shapes = [
        jax.ShapeDtypeStruct(tokens, BF16),
        jax.ShapeDtypeStruct(tokens, BF16),
        jax.ShapeDtypeStruct((384,), F32),
        jax.ShapeDtypeStruct((24, 72), F32),
        jax.ShapeDtypeStruct((24, 24), F32),
        jax.ShapeDtypeStruct((12, 2, 207), F32),
    ]
    outs = pl.pallas_call(
        kernel,
        out_shape=shapes,
        in_specs=[hbm] * 7 + [pl.BlockSpec(memory_space=pltpu.SMEM)] + [hbm] * len(consts),
        out_specs=[hbm] * 2 + [vmem] * 4,
        scratch_shapes=[
            pltpu.VMEM((384,), F32),
            pltpu.VMEM(qkv_weight.shape, BF16),
            pltpu.VMEM(proj_weight.shape, BF16),
            pltpu.VMEM((12, 32, 3312), BF16),
            pltpu.VMEM((6, 2, 12), jnp.int32),
        ]
        + [pltpu.VMEM(c.shape, BF16) for c in consts]
        + [
            pltpu.VMEM(tokens, BF16),
            pltpu.VMEM(tokens, BF16),
            pltpu.VMEM(tokens, BF16),
            pltpu.VMEM(tokens, BF16),
            pltpu.VMEM(tokens, BF16),
            pltpu.VMEM(tokens, BF16),
            pltpu.VMEM((144, 384), BF16),
            pltpu.VMEM((16, 128), F32),
            pltpu.VMEM((16, 3456), F32),
            pltpu.VMEM((192, 384), BF16),
            pltpu.VMEM((12, 144, 144), F32),
            pltpu.VMEM((3, 576, 144), F32),
            pltpu.VMEM((6, 288, 144), F32),
            pltpu.VMEM((3, 144, 256), BF16),
            pltpu.VMEM((144, 384), BF16),
            pltpu.VMEM((144, 384), BF16),
            pltpu.VMEM((192, 144), BF16),
            pltpu.VMEM((192, 144), BF16),
            pltpu.VMEM((192, 144), BF16),
            pltpu.VMEM((192, 144), BF16),
            pltpu.VMEM((192, 144), BF16),
            pltpu.VMEM((192, 144), BF16),
            pltpu.VMEM((3, 144, 256), BF16),
            pltpu.VMEM((144, 384), BF16),
            pltpu.VMEM((144, 384), BF16),
            pltpu.VMEM((144, 384), BF16),
            pltpu.VMEM((2, 4, 48, 384), BF16),
            pltpu.VMEM((2, 4, 48, 384), BF16),
            pltpu.VMEM((3, 8, 48, 128), BF16),
            pltpu.VMEM((3, 8, 48, 128), BF16),
            pltpu.VMEM((48, 384), BF16),
            pltpu.VMEM((48, 384), BF16),
            pltpu.VMEM((16, 32, 128), BF16),
            pltpu.VMEM((16, 32, 128), BF16),
            pltpu.VMEM((16, 16, 256), BF16),
            pltpu.VMEM((16, 16, 256), BF16),
            pltpu.VMEM((16, 256), BF16),
            pltpu.VMEM((16, 16, 256), BF16),
            dma((len(consts) + 5,)), dma((4,)),
            dma((6,)), dma((6,)), dma((6,)), dma((6,)), dma((7,)), dma((7,)),
            dma((2,)), dma((2,)), dma((3,)), dma((3,)), dma, dma,
            dma, dma, dma, dma, dma, dma,
        ],
        compiler_params=pltpu.CompilerParams(
            collective_id=0, has_side_effects=True, vmem_limit_bytes=62 * 2**20
        ),
    )(
        inputs.transpose(1, 2, 0, 3),
        cotangent.transpose(1, 2, 0, 3),
        norm_gain,
        qkv_weight,
        proj_weight,
        bias_table.transpose(1, 0, 2),
        region.transpose(1, 0, 2),
        window_type,
        *consts,
    )
    outs = pl.pallas_call(
        finish,
        out_shape=shapes,
        in_specs=[vmem] * 6,
        out_specs=[vmem] * 6,
    )(*outs)
    block_out, grad_inputs, grad_gain, grad_qkv, grad_proj, grad_bias = outs
    return (
        block_out.transpose(2, 0, 1, 3),
        grad_inputs.transpose(2, 0, 1, 3),
        grad_gain,
        grad_qkv,
        grad_proj,
        grad_bias.transpose(1, 0, 2),
    )


def solution(mesh):
    return jax.shard_map(
        local,
        mesh=mesh,
        in_specs=(
            P(None, "lat", "lon", None),
            P(None, "lat", "lon", None),
            P(),
            P(),
            P(),
            P(),
            P("lat", None),
            P(None, "lat", "lon"),
        ),
        out_specs=(
            P(None, "lat", "lon", None),
            P(None, "lat", "lon", None),
            P(),
            P("lat", "lon"),
            P("lat", "lon"),
            P("lat", None, "lon"),
        ),
        check_vma=False,
    )
```

```python
import functools

import jax
import jax.numpy as jnp
import numpy as np
from jax import lax
from jax.experimental import pallas as pl
from jax.experimental.pallas import tpu as pltpu
from jax.sharding import PartitionSpec as P

F32 = jnp.float32
BF16 = jnp.bfloat16
MESH = pl.DeviceIdType.MESH
SCALE = 32 ** (-0.5)


def patterns():
    order = np.zeros((144, 144), np.float32)
    toeplitz = np.zeros((6, 144, 768), np.float32)
    dup = np.zeros((2, 288, 192), np.float32)
    key_rows = np.zeros((144, 16), np.float32)
    key_cols = np.zeros((144, 128), np.float32)
    halves = np.zeros((384, 384), np.float32)
    for l in range(2):
        for r in range(6):
            for c in range(12):
                p = 12 * c + 6 * l + r
                order[p, 24 * r + 2 * c + l] = 1
                key_rows[p, 2 * ((r + 3) % 6) + 1 - l] = 1
                key_cols[p, (c + 6) % 12] = 1
                for m in range(6):
                    for par in range(2):
                        spot = (2 * m + par + 6) % 12 - (c + 6) % 12 + 11
                        iq = (r + 3) % 6
                        lane = (1 - l) * 138 + iq * 23 + spot
                        toeplitz[m, p, 384 * par + lane] = 1
    for h in range(12):
        for par in range(2):
            for l in range(2):
                for r in range(6):
                    zi = (1 - l) * 6 + (r + 3) % 6
                    dup[par, 24 * h + 12 * par + 6 * l + r, 16 * zi + h] = 1
    for f in range(384):
        i = f // 24
        halves[192 * (i % 2) + 24 * (i // 2) + f % 24, f] = 1
    both = [
        key_rows,
        key_cols,
        key_cols.T,
        dup,
        toeplitz,
        order,
        halves,
        order.T,
        dup.transpose(0, 2, 1),
    ]
    return [jnp.asarray(x, BF16) for x in both]


def dot(a, b, ca=1, cb=0):
    return lax.dot_general(a, b, (((ca,), (cb,)), ((), ())), preferred_element_type=F32)


def roll_left(value, by):
    width = value.shape[1]
    by = by % width
    return value if by == 0 else pltpu.roll(value, width - by, 1)


def kernel(
    in_hbm,
    cot_hbm,
    gain_hbm,
    wqkv_hbm,
    wproj_hbm,
    table_hbm,
    region_hbm,
    type_ref,
    *rest,
):
    const_hbm = rest[:9]
    out_ref, gin_ref, ggain_ref, gqkv_ref, gproj_ref, gbias_ref = rest[9:15]
    gain_ref, wqkv, wproj, table, region_ref = rest[15:20]
    const = rest[20:29]
    (
        win, win_cot, res, res_cot, out_own, gin_own, tok, keys, trow, amat, bias, probs, gsb, gqk, agv, hid,
        gqk_in, agv_in, hid_in, cw, cw_in,
        ysend, yrecv, zsend, zrecv, xsend, xrecv, lsend, lrecv, bsend, brecv, asend, arecv,
        load_sem, own_sem, halo_s, halo_r, back_s, back_r, sib_s, sib_r, y_s, y_r, z_s, z_r, x_s, x_r,
        l_s, l_r, b_s, b_r, a_s, a_r,
    ) = rest[29:]
    key_rows, key_cols, key_cols_t, dup, toep, order, halves, order_t, dup_t = const

    i = lax.axis_index("lat")
    j = lax.axis_index("lon")
    y, x, core = i // 4, (i // 2) % 2, i % 2
    sibling = (i + 1 - 2 * core, j)
    up, down = (i + 15) % 16, (i + 1) % 16
    left, right = (j + 15) % 16, (j + 1) % 16

    def remote(src, dst, ssem, rsem, dev):
        return pltpu.make_async_remote_copy(
            src_ref=src, dst_ref=dst, send_sem=ssem, recv_sem=rsem,
            device_id=dev, device_id_type=MESH,
        )

    barrier = pltpu.get_barrier_semaphore()
    for dev in ((up, left), (down, right)):
        pl.semaphore_signal(barrier, inc=1, device_id=dev, device_id_type=MESH)
    for d in (15, 1, *range(2, 15)):
        pl.semaphore_signal(barrier, inc=1, device_id=((i + d) % 16, j), device_id_type=MESH)
        pl.semaphore_signal(barrier, inc=1, device_id=(i, (j + d) % 16), device_id_type=MESH)

    own = [
        pltpu.make_async_copy(s.at[3:6, 6:12], d.at[3:6, 6:12], own_sem.at[n])
        for n, (s, d) in enumerate(((in_hbm, win), (cot_hbm, win_cot)))
    ]
    loads = [
        pltpu.make_async_copy(s, d, load_sem.at[n])
        for n, (s, d) in enumerate(
            zip(
                (region_hbm, *const_hbm[:3], table_hbm, *const_hbm[3:6], gain_hbm, wqkv_hbm, const_hbm[6], wproj_hbm, *const_hbm[7:]),
                (region_ref, *const[:3], table, *const[3:6], gain_ref, wqkv, const[6], wproj, *const[7:]),
            )
        )
    ]
    for c in (*own, *loads):
        c.start()

    corners = (
        ((slice(0, 3), slice(0, 6)), (up, left), (down, right)),
        ((slice(0, 3), slice(6, 12)), (up, j), (down, j)),
        ((slice(3, 6), slice(0, 6)), (i, left), (i, right)),
    )
    halo = [
        remote(s.at[spot], d.at[spot], halo_s.at[3 * n + k], halo_r.at[3 * n + k], dev)
        for n, (s, d) in enumerate(((in_hbm, win), (cot_hbm, win_cot)))
        for k, (spot, dev, _) in enumerate(corners)
    ]
    pl.semaphore_wait(barrier, 32)
    for c in halo:
        c.start()

    for c in loads[0:4]:
        c.wait()
    for n in range(6):
        lat_side = (6 * i + n + 3 >= 96).astype(jnp.int32) * 2
        level = lax.broadcasted_iota(jnp.int32, (2, 12), 0)
        keys[2 * n : 2 * n + 2, 0:12] = (region_ref[n] * 4 + lat_side + level).astype(F32)
    in_grid = (lax.broadcasted_iota(jnp.int32, (16, 128), 0) < 12) & (
        lax.broadcasted_iota(jnp.int32, (16, 128), 1) < 12
    )
    key_grid = jnp.where(in_grid, keys[...], 0.0).astype(BF16)
    key_p = jnp.sum(
        dot(key_rows[...], key_grid) * key_cols[...].astype(F32), 1, keepdims=True
    )
    key_q = jnp.sum(
        dot(key_grid, key_rows[...], 0, 1) * key_cols_t[...].astype(F32), 0, keepdims=True
    )
    allowed = key_p == key_q

    kind = type_ref[0, 0]
    trow[...] = jnp.zeros((16, 3456), F32)
    is_kind = lax.broadcasted_iota(jnp.int32, (32, 3312), 0) == kind
    loads[4].wait()
    for h in range(12):
        trow[h : h + 1, 0:3312] = jnp.sum(
            jnp.where(is_kind, table[h].astype(F32), 0.0), 0, keepdims=True
        )
    wide_lane = lax.broadcasted_iota(jnp.int32, (16, 384), 1)
    for zp in range(2):
        for ip in range(6):
            pieces = []
            for zq in range(2):
                off = ((2 * zp + zq) * 36 + 6 * ip) * 23
                a = off // 128 * 128
                pieces.append(roll_left(trow[:, a : a + 384], off - a - 138 * zq))
            row = (6 * zp + ip) * 16
            amat[row : row + 16, :] = jnp.where(wide_lane < 138, *pieces).astype(BF16)
    loads[5].wait()
    spread = jnp.concatenate([dot(dup[0], amat[...]), dot(dup[1], amat[...])], 1).astype(BF16)
    loads[6].wait()
    for m in range(6):
        part = dot(spread, toep[m], 1, 1)
        ok = allowed[24 * m : 24 * m + 24]
        for h in range(12):
            bias[h, 24 * m : 24 * m + 24, :] = jnp.where(ok, part[24 * h : 24 * h + 24], -1e30)
    for c in loads[7:]:
        c.wait()

    def gather(source):
        for r in range(6):
            for c in range(12):
                k = 24 * r + 2 * c
                tok[k : k + 2, :] = source[r, c]
        return dot(order[...], tok[...])


    own[0].wait()
    for c in halo[0:3]:
        c.wait_recv()
    wide = gather(win)
    to_sib = [
        remote(src, dst, sib_s.at[n], sib_r.at[n], sibling)
        for n, (src, dst) in enumerate(
            [(cw, cw_in), (hid, hid_in)]
            + [(agv.at[g], agv_in.at[g]) for g in range(3)]
            + [(gqk.at[g], gqk_in.at[g]) for g in range(3)]
        )
    ]

    def own_half(value):
        picked = halves[pl.ds(pl.multiple_of(192 * core, 192), 192), :]
        return dot(picked, value, 1, 1).astype(BF16)

    def whole(ref, ssem, rsem):
        return [pltpu.make_async_copy(ref, ref, sem) for sem in (ssem, rsem)]

    def weight_part(n, left_own, left_in, right_own, right_in):
        part = dot(left_own, right_own) + dot(left_in, right_in)
        if n >= 2:
            q = n - 2
            for k in range(8):
                rows = part[24 * k : 24 * k + 24]
                zsend[q, k] = jnp.concatenate([rows[:, 0:128], rows[:, 128:256]], 0).astype(BF16)

            def to_lat(d):
                k = 2 * ((y + d // 2) % 4) + (x + d) % 2
                return remote(
                    zsend.at[q, k], zrecv.at[q, d], z_s.at[q], z_r.at[q], (2 * k + core, j)
                )

            parts = [to_lat(d) for d in range(1, 8)]
            waits = whole(zrecv.at[q, pl.ds(1, 7)], z_s.at[q], z_r.at[q])
        else:
            for k in range(4):
                ysend[n, k] = part[48 * k : 48 * k + 48].astype(BF16)

            def to_y(d):
                k = (y + d) % 4
                return remote(
                    ysend.at[n, k], yrecv.at[n, d], y_s.at[n], y_r.at[n],
                    (4 * k + 2 * x + core, j),
                )

            parts = [to_y(d) for d in range(1, 4)]
            waits = whole(yrecv.at[n, pl.ds(1, 3)], y_s.at[n], y_r.at[n])
        for c in parts:
            c.start()
        return waits

    def over_x():
        keep, others = [], []
        for n in range(2):
            y_copies[n][1].wait()
            chunk = ysend[n, y].astype(F32)
            for d in range(1, 4):
                chunk = chunk + yrecv[n, d].astype(F32)
            keep.append(jnp.where(x == 0, chunk[0:24], chunk[24:48]))
            others.append(jnp.where(x == 0, chunk[24:48], chunk[0:24]))
        xsend[...] = jnp.concatenate(others, 0).astype(BF16)
        to_x = remote(xsend, xrecv, x_s, x_r, (4 * y + 2 * (1 - x) + core, j))
        to_x.start()
        return keep, to_x

    landed = (out_own, gin_own)

    def put_back(value, target, n):
        back_rows = dot(order_t[...], value).astype(BF16)
        for r in range(6):
            for c in range(12):
                k = 24 * r + 2 * c
                kept = r >= 3 and c >= 6
                (landed[n] if kept else target)[r, c] = back_rows[k : k + 2]
        sends = [
            remote(
                target.at[spot], landed[n].at[spot],
                back_s.at[3 * n + k], back_r.at[3 * n + k], dev,
            )
            for k, (spot, _, dev) in enumerate(corners)
        ]
        for c in sends:
            c.start()
        return sends

    gain = gain_ref[...].reshape(1, 384)
    center = jnp.mean(wide, 1, keepdims=True)
    shifted = wide - center
    inv_std = lax.rsqrt(jnp.mean(jnp.square(shifted), 1, keepdims=True) + 1e-05)
    normed = shifted * inv_std
    hidden = (normed * gain).astype(BF16)
    hid[...] = hidden
    to_sib[1].start()
    joined = dot(hidden, wqkv[...]).astype(BF16)
    hidden_own = own_half(hidden)
    own[1].wait()
    for c in halo[3:6]:
        c.wait_recv()
    cw[...] = gather(win_cot).astype(BF16)
    to_sib[0].start()
    cot_rows = cw[...]
    grad_att = dot(cot_rows, wproj[...], 1, 1).astype(BF16)

    lane_head = lax.broadcasted_iota(jnp.int32, (1, 128), 1) // 32
    head_masks = [(lane_head == h).astype(F32).astype(BF16) for h in range(4)]
    wide_masks = [(lane_head == h).astype(F32) for h in range(4)]

    def pick(stacked):
        total = stacked[0:144] * wide_masks[0]
        for h in range(1, 4):
            total = total + stacked[144 * h : 144 * h + 144] * wide_masks[h]
        return total

    for g in range(3):
        lanes = slice(128 * g, 128 * g + 128)
        queries4 = jnp.concatenate([joined[:, lanes] * k for k in head_masks], 0)
        key_part = joined[:, 384 + 128 * g : 384 + 128 * g + 128]
        value_part = joined[:, 768 + 128 * g : 768 + 128 * g + 128]
        scores = dot(queries4, key_part, 1, 1) * SCALE
        scores = scores + bias[4 * g : 4 * g + 4].reshape(576, 144)
        top = jnp.max(scores, 1, keepdims=True)
        weights = jnp.exp(scores - top)
        weights = weights * (1.0 / jnp.sum(weights, 1, keepdims=True))
        probs[g] = weights
        probs_low = weights.astype(BF16)
        agv[g, :, 0:128] = pick(dot(probs_low, value_part)).astype(BF16)
        grad4 = jnp.concatenate([grad_att[:, lanes] * k for k in head_masks], 0)
        agv[g, :, 128:256] = dot(probs_low, grad4, 0, 0).astype(BF16)
        to_sib[2 + g].start()
    attended = jnp.concatenate([agv[g, :, 0:128] for g in range(3)], 1)
    grad_values = jnp.concatenate([agv[g, :, 128:256] for g in range(3)], 1)
    attended_own = own_half(attended)
    to_sib[1].wait_recv()
    hidden_in = own_half(hid_in[...])

    result = (wide + dot(attended, wproj[...])).astype(BF16)
    back_out = put_back(result, res, 0)

    for g in range(3):
        to_sib[2 + g].wait_recv()
    values_in = jnp.concatenate([agv_in[g, :, 128:256] for g in range(3)], 1)
    y_copies = [weight_part(0, hidden_own, hidden_in, grad_values, values_in)]
    to_sib[0].wait_recv()
    attended_in = own_half(jnp.concatenate([agv_in[g, :, 0:128] for g in range(3)], 1))
    y_copies.append(weight_part(1, attended_own, attended_in, cw[...], cw_in[...]))
    for g in range(3):
        lanes = slice(128 * g, 128 * g + 128)
        queries4 = jnp.concatenate([joined[:, lanes] * k for k in head_masks], 0)
        key_part = joined[:, 384 + 128 * g : 384 + 128 * g + 128]
        value_part = joined[:, 768 + 128 * g : 768 + 128 * g + 128]
        grad4 = jnp.concatenate([grad_att[:, lanes] * k for k in head_masks], 0)
        weights = probs[g]
        grad_probs = dot(grad4, value_part, 1, 1)
        grad_scores = weights * (grad_probs - jnp.sum(weights * grad_probs, 1, keepdims=True))
        for h in range(4):
            for m in range(6):
                row = 24 * (4 * g + h)
                gsb[m, row : row + 24, :] = grad_scores[144 * h + 24 * m : 144 * h + 24 * m + 24]
        grad_scaled = (grad_scores * SCALE).astype(BF16)
        grad_query = pick(dot(grad_scaled, key_part))
        grad_keys = dot(grad_scaled, queries4, 0, 0)
        gqk[g, :, 0:128] = grad_query.astype(BF16)
        gqk[g, :, 128:256] = grad_keys.astype(BF16)
        to_sib[5 + g].start()
        if g > 0:
            to_sib[4 + g].wait_recv()
            y_copies.append(weight_part(1 + g, hidden_own, hidden_in, gqk[g - 1], gqk_in[g - 1]))

    grad_joined = jnp.concatenate(
        [gqk[g, :, 128 * n : 128 * n + 128] for n in range(2) for g in range(3)] + [grad_values], 1
    )
    grad_hidden = dot(grad_joined, wqkv[...], 1, 1)
    grad_gain = jnp.sum(grad_hidden * normed, 0, keepdims=True)
    folded = dot(gsb[0].astype(BF16), toep[0])
    for m in range(1, 6):
        folded = folded + dot(gsb[m].astype(BF16), toep[m])
    folded = folded.astype(BF16)

    shares = dot(dup_t[0], folded[:, 0:384]) + dot(dup_t[1], folded[:, 384:768])
    share_row = lax.broadcasted_iota(jnp.int32, (16, 256), 0)
    share_lane = lax.broadcasted_iota(jnp.int32, (16, 256), 1)

    def riders(gain_row, kind_row):
        high = gain_row.astype(BF16).astype(F32)
        low = gain_row - high
        rows = [
            high[:, 0:256],
            jnp.concatenate([high[:, 256:384], jnp.zeros((1, 128), F32)], 1),
            low[:, 0:256],
            jnp.concatenate([low[:, 256:384], jnp.zeros((1, 128), F32)], 1),
        ]
        block = jnp.where((share_row == 15) & (share_lane >= 128), kind_row, 0.0)
        for n, row in enumerate(rows):
            block = block + jnp.where(share_row == 12 + n, row, 0.0)
        return block

    def gain_of(block):
        return jnp.concatenate(
            [block[12:13] + block[14:15], block[13:14, 0:128] + block[15:16, 0:128]], 1
        )

    extra = riders(grad_gain, kind.astype(F32))
    for dest in range(16):
        zp, zq, k = dest // 8, (dest // 4) % 2, dest % 4
        first = (6 * zp + 3 * k // 2) * 16
        edge = 69 if k % 2 else 138
        pieces = [
            roll_left(shares[row : row + 16], 138 * zq + start)[:, 0:256]
            for row, start in ((first, 138 - edge), (first + 16, -edge))
        ]
        block = jnp.where(share_lane < edge, *pieces)
        block = jnp.where((share_row < 12) & (share_lane < 207), block, 0.0) + extra
        bsend[dest] = block.astype(BF16)

    def bias_lon(d):
        to = (j + d) % 16
        return remote(bsend.at[to], brecv.at[d], b_s, b_r, (i, to))

    def start_all(make):
        def body(d, carry):
            make(d).start()
            return carry

        lax.fori_loop(1, 16, body, 0)

    all_lon = whole(lrecv.at[pl.ds(1, 15)], l_s, l_r)
    all_bias = whole(brecv.at[pl.ds(1, 15)], b_s, b_r)
    all_lat = whole(arecv.at[pl.ds(1, 15)], a_s, a_r)
    start_all(bias_lon)

    to_sib[7].wait_recv()
    y_copies.append(weight_part(4, hidden_own, hidden_in, gqk[2], gqk_in[2]))

    mine, to_x = over_x()
    grad_normed = grad_hidden * gain
    grad_wide = inv_std * (
        grad_normed
        - jnp.mean(grad_normed, 1, keepdims=True)
        - normed * jnp.mean(grad_normed * normed, 1, keepdims=True)
    )
    grad_in = (cot_rows.astype(F32) + grad_wide).astype(BF16)
    back_grad = put_back(grad_in, res_cot, 1)

    all_bias[1].wait()
    total = bsend[j].astype(F32)
    for d in range(1, 16):
        total = total + brecv[d].astype(F32)
    kinds = total[15:16, 128:129] * (1.0 / 16.0)
    block = jnp.where(share_row < 12, total, 0.0) + riders(gain_of(total), kinds)
    asend[...] = block.astype(BF16)

    def bias_lat(d):
        return remote(asend, arecv.at[d], a_s, a_r, ((i + d) % 16, j))

    start_all(bias_lat)

    own_qk = []
    for q in range(3):
        y_copies[2 + q][1].wait()
        chunk = zsend[q, 2 * y + x].astype(F32)
        for d in range(1, 8):
            chunk = chunk + zrecv[q, d].astype(F32)
        own_qk.append(chunk)
    to_x.wait_recv()
    got = xrecv[...].astype(F32)
    own_value = mine[0] + got[0:24]
    own_proj = mine[1] + got[24:48]
    own_qkv = jnp.concatenate(
        [part[0:24] for part in own_qk] + [part[24:48] for part in own_qk] + [own_value],
        1,
    )
    lane128 = lax.broadcasted_iota(jnp.int32, (24, 128), 1)
    for dest in range(16):
        off = 72 * dest
        a = min(off // 128 * 128, 896)
        piece = roll_left(own_qkv[:, a : a + 256], off - a)[:, :128]
        off = 24 * dest
        a = min(off // 128 * 128, 128)
        tail = roll_left(own_proj[:, a : a + 256], off - a - 72)[:, :128]
        block = jnp.where(lane128 < 72, piece, tail)
        block = jnp.concatenate([block, jnp.zeros((8, 128), F32)], 0)
        lsend[dest] = block.astype(BF16)

    def to_lon(d):
        to = (j + d) % 16
        return remote(lsend.at[to], lrecv.at[d], l_s, l_r, (i, to))

    start_all(to_lon)


    for c in (*halo, *to_sib, *back_out, *back_grad, to_x):
        c.wait_send()
    for sent, _ in y_copies:
        sent.wait()
    all_bias[0].wait()

    writes = []
    for n, (copies, target) in enumerate(((back_out, out_ref), (back_grad, gin_ref))):
        for c in copies:
            c.wait_recv()
        writes.append(pltpu.make_async_copy(landed[n], target, own_sem.at[2 + n]))
        writes[n].start()

    all_lat[1].wait()
    gain_total = jnp.zeros((1, 384), F32)
    sums = [jnp.zeros((16, 256), F32), jnp.zeros((16, 256), F32)]
    for d in range(16):
        block = asend[...] if d == 0 else arecv[d]
        block = block.astype(F32)
        gain_total = gain_total + gain_of(block)
        for t in range(2):
            hit = block[15:16, 128:129] == (2 * i + t).astype(F32)
            sums[t] = sums[t] + jnp.where(hit, block, 0.0)
    ggain_ref[...] = gain_total.reshape(384)
    for h in range(12):
        row = jnp.concatenate([sums[0][h : h + 1, 0:207], sums[1][h : h + 1, 0:207]], 0)
        gbias_ref[h] = row
    all_lat[0].wait()

    all_lon[1].wait()
    total = lsend[j].astype(F32)
    for d in range(1, 16):
        total = total + lrecv[d].astype(F32)
    gqkv_ref[...] = total[0:24, 0:72]
    gproj_ref[...] = roll_left(total[0:24], 72)[:, 0:24]
    all_lon[0].wait()
    for c in writes:
        c.wait()


def finish(*refs):
    for source, target in zip(refs[:6], refs[6:]):
        target[...] = source[...]


def local(inputs, cotangent, norm_gain, qkv_weight, proj_weight, bias_table, window_type, region):
    consts = patterns()
    vmem = pl.BlockSpec(memory_space=pltpu.VMEM)
    hbm = pl.BlockSpec(memory_space=pltpu.HBM)
    dma = pltpu.SemaphoreType.DMA
    tokens = (6, 12, 2, 384)
    shapes = [
        jax.ShapeDtypeStruct(tokens, BF16),
        jax.ShapeDtypeStruct(tokens, BF16),
        jax.ShapeDtypeStruct((384,), F32),
        jax.ShapeDtypeStruct((24, 72), F32),
        jax.ShapeDtypeStruct((24, 24), F32),
        jax.ShapeDtypeStruct((12, 2, 207), F32),
    ]
    outs = pl.pallas_call(
        kernel,
        out_shape=shapes,
        in_specs=[hbm] * 7 + [pl.BlockSpec(memory_space=pltpu.SMEM)] + [hbm] * len(consts),
        out_specs=[hbm] * 2 + [vmem] * 4,
        scratch_shapes=[
            pltpu.VMEM((384,), F32),
            pltpu.VMEM(qkv_weight.shape, BF16),
            pltpu.VMEM(proj_weight.shape, BF16),
            pltpu.VMEM((12, 32, 3312), BF16),
            pltpu.VMEM((6, 2, 12), jnp.int32),
        ]
        + [pltpu.VMEM(c.shape, BF16) for c in consts]
        + [
            pltpu.VMEM(tokens, BF16),
            pltpu.VMEM(tokens, BF16),
            pltpu.VMEM(tokens, BF16),
            pltpu.VMEM(tokens, BF16),
            pltpu.VMEM(tokens, BF16),
            pltpu.VMEM(tokens, BF16),
            pltpu.VMEM((144, 384), BF16),
            pltpu.VMEM((16, 128), F32),
            pltpu.VMEM((16, 3456), F32),
            pltpu.VMEM((192, 384), BF16),
            pltpu.VMEM((12, 144, 144), F32),
            pltpu.VMEM((3, 576, 144), F32),
            pltpu.VMEM((6, 288, 144), F32),
            pltpu.VMEM((3, 144, 256), BF16),
            pltpu.VMEM((3, 144, 256), BF16),
            pltpu.VMEM((144, 384), BF16),
            pltpu.VMEM((3, 144, 256), BF16),
            pltpu.VMEM((3, 144, 256), BF16),
            pltpu.VMEM((144, 384), BF16),
            pltpu.VMEM((144, 384), BF16),
            pltpu.VMEM((144, 384), BF16),
            pltpu.VMEM((2, 4, 48, 384), BF16),
            pltpu.VMEM((2, 4, 48, 384), BF16),
            pltpu.VMEM((3, 8, 48, 128), BF16),
            pltpu.VMEM((3, 8, 48, 128), BF16),
            pltpu.VMEM((48, 384), BF16),
            pltpu.VMEM((48, 384), BF16),
            pltpu.VMEM((16, 32, 128), BF16),
            pltpu.VMEM((16, 32, 128), BF16),
            pltpu.VMEM((16, 16, 256), BF16),
            pltpu.VMEM((16, 16, 256), BF16),
            pltpu.VMEM((16, 256), BF16),
            pltpu.VMEM((16, 16, 256), BF16),
            dma((len(consts) + 5,)), dma((4,)),
            dma((6,)), dma((6,)), dma((6,)), dma((6,)), dma((8,)), dma((8,)),
            dma((2,)), dma((2,)), dma((3,)), dma((3,)), dma, dma,
            dma, dma, dma, dma, dma, dma,
        ],
        compiler_params=pltpu.CompilerParams(
            collective_id=0, has_side_effects=True, vmem_limit_bytes=62 * 2**20
        ),
    )(
        inputs.transpose(1, 2, 0, 3),
        cotangent.transpose(1, 2, 0, 3),
        norm_gain,
        qkv_weight,
        proj_weight,
        bias_table.transpose(1, 0, 2),
        region.transpose(1, 0, 2),
        window_type,
        *consts,
    )
    outs = pl.pallas_call(
        finish,
        out_shape=shapes,
        in_specs=[vmem] * 6,
        out_specs=[vmem] * 6,
    )(*outs)
    block_out, grad_inputs, grad_gain, grad_qkv, grad_proj, grad_bias = outs
    return (
        block_out.transpose(2, 0, 1, 3),
        grad_inputs.transpose(2, 0, 1, 3),
        grad_gain,
        grad_qkv,
        grad_proj,
        grad_bias.transpose(1, 0, 2),
    )


def solution(mesh):
    return jax.shard_map(
        local,
        mesh=mesh,
        in_specs=(
            P(None, "lat", "lon", None),
            P(None, "lat", "lon", None),
            P(),
            P(),
            P(),
            P(),
            P("lat", None),
            P(None, "lat", "lon"),
        ),
        out_specs=(
            P(None, "lat", "lon", None),
            P(None, "lat", "lon", None),
            P(),
            P("lat", "lon"),
            P("lat", "lon"),
            P("lat", None, "lon"),
        ),
        check_vma=False,
    )
```

```python
import functools

import jax
import jax.numpy as jnp
import numpy as np
from jax import lax
from jax.experimental import pallas as pl
from jax.experimental.pallas import tpu as pltpu
from jax.sharding import PartitionSpec as P

F32 = jnp.float32
BF16 = jnp.bfloat16
MESH = pl.DeviceIdType.MESH
SCALE = 32 ** (-0.5)


def patterns():
    order = np.zeros((144, 144), np.float32)
    toeplitz = np.zeros((6, 144, 768), np.float32)
    dup = np.zeros((2, 288, 192), np.float32)
    key_rows = np.zeros((144, 16), np.float32)
    key_cols = np.zeros((144, 128), np.float32)
    halves = np.zeros((384, 384), np.float32)
    for l in range(2):
        for r in range(6):
            for c in range(12):
                p = 12 * c + 6 * l + r
                order[p, 24 * r + 2 * c + l] = 1
                key_rows[p, 2 * ((r + 3) % 6) + 1 - l] = 1
                key_cols[p, (c + 6) % 12] = 1
                for m in range(6):
                    for par in range(2):
                        spot = (2 * m + par + 6) % 12 - (c + 6) % 12 + 11
                        iq = (r + 3) % 6
                        lane = (1 - l) * 138 + iq * 23 + spot
                        toeplitz[m, p, 384 * par + lane] = 1
    for h in range(12):
        for par in range(2):
            for l in range(2):
                for r in range(6):
                    zi = (1 - l) * 6 + (r + 3) % 6
                    dup[par, 24 * h + 12 * par + 6 * l + r, 16 * zi + h] = 1
    for f in range(384):
        i = f // 24
        halves[192 * (i % 2) + 24 * (i // 2) + f % 24, f] = 1
    both = [
        key_rows,
        key_cols,
        key_cols.T,
        dup,
        toeplitz,
        order,
        halves,
        order.T,
        dup.transpose(0, 2, 1),
    ]
    return [jnp.asarray(x, BF16) for x in both]


def dot(a, b, ca=1, cb=0):
    return lax.dot_general(a, b, (((ca,), (cb,)), ((), ())), preferred_element_type=F32)


def roll_left(value, by):
    width = value.shape[1]
    by = by % width
    return value if by == 0 else pltpu.roll(value, width - by, 1)


def kernel(
    in_hbm,
    cot_hbm,
    gain_hbm,
    wqkv_hbm,
    wproj_hbm,
    table_hbm,
    region_hbm,
    type_ref,
    *rest,
):
    const_hbm = rest[:9]
    out_ref, gin_ref, ggain_ref, gqkv_ref, gproj_ref, gbias_ref = rest[9:15]
    gain_ref, wqkv, wproj, table, region_ref = rest[15:20]
    const = rest[20:29]
    (
        win, win_cot, res, res_cot, out_own, gin_own, tok, keys, trow, amat, bias, probs, gsb, gqk, agv, hid,
        gqk_in, agv_in, hid_in, cw, cw_in,
        ysend, yrecv, zsend, zrecv, xsend, xrecv, lsend, lrecv, bsend, brecv, asend, arecv,
        load_sem, own_sem, halo_s, halo_r, back_s, back_r, sib_s, sib_r, y_s, y_r, z_s, z_r, x_s, x_r,
        l_s, l_r, b_s, b_r, a_s, a_r,
    ) = rest[29:]
    key_rows, key_cols, key_cols_t, dup, toep, order, halves, order_t, dup_t = const

    i = lax.axis_index("lat")
    j = lax.axis_index("lon")
    y, x, core = i // 4, (i // 2) % 2, i % 2
    sibling = (i + 1 - 2 * core, j)
    up, down = (i + 15) % 16, (i + 1) % 16
    left, right = (j + 15) % 16, (j + 1) % 16

    def remote(src, dst, ssem, rsem, dev):
        return pltpu.make_async_remote_copy(
            src_ref=src, dst_ref=dst, send_sem=ssem, recv_sem=rsem,
            device_id=dev, device_id_type=MESH,
        )

    barrier = pltpu.get_barrier_semaphore()
    for dev in ((up, left), (down, right)):
        pl.semaphore_signal(barrier, inc=1, device_id=dev, device_id_type=MESH)
    for d in (15, 1, *range(2, 15)):
        pl.semaphore_signal(barrier, inc=1, device_id=((i + d) % 16, j), device_id_type=MESH)
        pl.semaphore_signal(barrier, inc=1, device_id=(i, (j + d) % 16), device_id_type=MESH)

    own = [
        pltpu.make_async_copy(s.at[3:6, 6:12], d.at[3:6, 6:12], own_sem.at[n])
        for n, (s, d) in enumerate(((in_hbm, win), (cot_hbm, win_cot)))
    ]
    loads = [
        pltpu.make_async_copy(s, d, load_sem.at[n])
        for n, (s, d) in enumerate(
            zip(
                (region_hbm, *const_hbm[:3], table_hbm, *const_hbm[3:6], gain_hbm, wqkv_hbm, const_hbm[6], wproj_hbm, *const_hbm[7:]),
                (region_ref, *const[:3], table, *const[3:6], gain_ref, wqkv, const[6], wproj, *const[7:]),
            )
        )
    ]
    for c in (*own, *loads[:7]):
        c.start()

    corners = (
        ((slice(0, 3), slice(0, 6)), (up, left), (down, right)),
        ((slice(0, 3), slice(6, 12)), (up, j), (down, j)),
        ((slice(3, 6), slice(0, 6)), (i, left), (i, right)),
    )
    halo = [
        remote(s.at[spot], d.at[spot], halo_s.at[3 * n + k], halo_r.at[3 * n + k], dev)
        for n, (s, d) in enumerate(((in_hbm, win), (cot_hbm, win_cot)))
        for k, (spot, dev, _) in enumerate(corners)
    ]
    pl.semaphore_wait(barrier, 32)
    for c in halo[0:3]:
        c.start()
    for c in loads[7:]:
        c.start()
    for c in halo[3:6]:
        c.start()

    for c in loads[0:4]:
        c.wait()
    for n in range(6):
        lat_side = (6 * i + n + 3 >= 96).astype(jnp.int32) * 2
        level = lax.broadcasted_iota(jnp.int32, (2, 12), 0)
        keys[2 * n : 2 * n + 2, 0:12] = (region_ref[n] * 4 + lat_side + level).astype(F32)
    in_grid = (lax.broadcasted_iota(jnp.int32, (16, 128), 0) < 12) & (
        lax.broadcasted_iota(jnp.int32, (16, 128), 1) < 12
    )
    key_grid = jnp.where(in_grid, keys[...], 0.0).astype(BF16)
    key_p = jnp.sum(
        dot(key_rows[...], key_grid) * key_cols[...].astype(F32), 1, keepdims=True
    )
    key_q = jnp.sum(
        dot(key_grid, key_rows[...], 0, 1) * key_cols_t[...].astype(F32), 0, keepdims=True
    )
    allowed = key_p == key_q

    kind = type_ref[0, 0]
    trow[...] = jnp.zeros((16, 3456), F32)
    pick_col = lax.broadcasted_iota(jnp.int32, (16, 384), 1)
    pick_row = lax.broadcasted_iota(jnp.int32, (16, 384), 0)
    is_kind = ((pick_col == 32 * pick_row + kind) & (pick_row < 12)).astype(F32).astype(BF16)
    loads[4].wait()
    trow[:, 0:3312] = dot(is_kind, table[...].reshape(384, 3312))
    wide_lane = lax.broadcasted_iota(jnp.int32, (16, 384), 1)
    for zp in range(2):
        for ip in range(6):
            pieces = []
            for zq in range(2):
                off = ((2 * zp + zq) * 36 + 6 * ip) * 23
                a = off // 128 * 128
                pieces.append(roll_left(trow[:, a : a + 384], off - a - 138 * zq))
            row = (6 * zp + ip) * 16
            amat[row : row + 16, :] = jnp.where(wide_lane < 138, *pieces).astype(BF16)
    loads[5].wait()
    spread = jnp.concatenate([dot(dup[0], amat[...]), dot(dup[1], amat[...])], 1).astype(BF16)
    loads[6].wait()
    for m in range(6):
        part = dot(spread, toep[m], 1, 1)
        ok = allowed[24 * m : 24 * m + 24]
        for h in range(12):
            bias[h, 24 * m : 24 * m + 24, :] = jnp.where(ok, part[24 * h : 24 * h + 24], -1e30)
    for c in loads[7:]:
        c.wait()

    def gather(source):
        for r in range(6):
            for c in range(12):
                k = 24 * r + 2 * c
                tok[k : k + 2, :] = source[r, c]
        return dot(order[...], tok[...])


    own[0].wait()
    for c in halo[0:3]:
        c.wait_recv()
    wide = gather(win)
    to_sib = [
        remote(src, dst, sib_s.at[n], sib_r.at[n], sibling)
        for n, (src, dst) in enumerate(
            [(cw, cw_in), (hid, hid_in)]
            + [(agv.at[g], agv_in.at[g]) for g in range(3)]
            + [(gqk.at[g], gqk_in.at[g]) for g in range(3)]
        )
    ]

    def own_half(value):
        picked = halves[pl.ds(pl.multiple_of(192 * core, 192), 192), :]
        return dot(picked, value, 1, 1).astype(BF16)

    def whole(ref, ssem, rsem):
        return [pltpu.make_async_copy(ref, ref, sem) for sem in (ssem, rsem)]

    def weight_part(n, left_own, left_in, right_own, right_in):
        part = dot(left_own, right_own) + dot(left_in, right_in)
        if n >= 2:
            q = n - 2
            for k in range(8):
                rows = part[24 * k : 24 * k + 24]
                zsend[q, k] = jnp.concatenate([rows[:, 0:128], rows[:, 128:256]], 0).astype(BF16)

            def to_lat(d):
                k = 2 * ((y + d // 2) % 4) + (x + d) % 2
                return remote(
                    zsend.at[q, k], zrecv.at[q, d], z_s.at[q], z_r.at[q], (2 * k + core, j)
                )

            parts = [to_lat(d) for d in range(1, 8)]
            waits = whole(zrecv.at[q, pl.ds(1, 7)], z_s.at[q], z_r.at[q])
        else:
            for k in range(4):
                ysend[n, k] = part[48 * k : 48 * k + 48].astype(BF16)

            def to_y(d):
                k = (y + d) % 4
                return remote(
                    ysend.at[n, k], yrecv.at[n, d], y_s.at[n], y_r.at[n],
                    (4 * k + 2 * x + core, j),
                )

            parts = [to_y(d) for d in range(1, 4)]
            waits = whole(yrecv.at[n, pl.ds(1, 3)], y_s.at[n], y_r.at[n])
        for c in parts:
            c.start()
        return waits

    def over_x():
        keep, others = [], []
        for n in range(2):
            y_copies[n][1].wait()
            chunk = ysend[n, y].astype(F32)
            for d in range(1, 4):
                chunk = chunk + yrecv[n, d].astype(F32)
            keep.append(jnp.where(x == 0, chunk[0:24], chunk[24:48]))
            others.append(jnp.where(x == 0, chunk[24:48], chunk[0:24]))
        xsend[...] = jnp.concatenate(others, 0).astype(BF16)
        to_x = remote(xsend, xrecv, x_s, x_r, (4 * y + 2 * (1 - x) + core, j))
        to_x.start()
        return keep, to_x

    landed = (out_own, gin_own)

    def put_back(value, target, n):
        back_rows = dot(order_t[...], value).astype(BF16)
        for r in range(6):
            for c in range(12):
                k = 24 * r + 2 * c
                kept = r >= 3 and c >= 6
                (landed[n] if kept else target)[r, c] = back_rows[k : k + 2]
        sends = [
            remote(
                target.at[spot], landed[n].at[spot],
                back_s.at[3 * n + k], back_r.at[3 * n + k], dev,
            )
            for k, (spot, _, dev) in enumerate(corners)
        ]
        for c in sends:
            c.start()
        return sends

    gain = gain_ref[...].reshape(1, 384)
    center = jnp.mean(wide, 1, keepdims=True)
    shifted = wide - center
    inv_std = lax.rsqrt(jnp.mean(jnp.square(shifted), 1, keepdims=True) + 1e-05)
    normed = shifted * inv_std
    hidden = (normed * gain).astype(BF16)
    hid[...] = hidden
    to_sib[1].start()
    joined = dot(hidden, wqkv[...]).astype(BF16)
    hidden_own = own_half(hidden)
    own[1].wait()
    for c in halo[3:6]:
        c.wait_recv()
    cw[...] = gather(win_cot).astype(BF16)
    to_sib[0].start()
    cot_rows = cw[...]
    grad_att = dot(cot_rows, wproj[...], 1, 1).astype(BF16)

    lane_head = lax.broadcasted_iota(jnp.int32, (1, 128), 1) // 32
    head_masks = [(lane_head == h).astype(F32).astype(BF16) for h in range(4)]
    wide_masks = [(lane_head == h).astype(F32) for h in range(4)]

    def pick(stacked):
        total = stacked[0:144] * wide_masks[0]
        for h in range(1, 4):
            total = total + stacked[144 * h : 144 * h + 144] * wide_masks[h]
        return total

    for g in range(3):
        lanes = slice(128 * g, 128 * g + 128)
        queries4 = jnp.concatenate([joined[:, lanes] * k for k in head_masks], 0)
        key_part = joined[:, 384 + 128 * g : 384 + 128 * g + 128]
        value_part = joined[:, 768 + 128 * g : 768 + 128 * g + 128]
        scores = dot(queries4, key_part, 1, 1) * SCALE
        scores = scores + bias[4 * g : 4 * g + 4].reshape(576, 144)
        top = jnp.max(scores, 1, keepdims=True)
        weights = jnp.exp(scores - top)
        weights = weights * (1.0 / jnp.sum(weights, 1, keepdims=True))
        probs[g] = weights
        probs_low = weights.astype(BF16)
        agv[g, :, 0:128] = pick(dot(probs_low, value_part)).astype(BF16)
        grad4 = jnp.concatenate([grad_att[:, lanes] * k for k in head_masks], 0)
        agv[g, :, 128:256] = dot(probs_low, grad4, 0, 0).astype(BF16)
        to_sib[2 + g].start()
    attended = jnp.concatenate([agv[g, :, 0:128] for g in range(3)], 1)
    grad_values = jnp.concatenate([agv[g, :, 128:256] for g in range(3)], 1)
    attended_own = own_half(attended)
    to_sib[1].wait_recv()
    hidden_in = own_half(hid_in[...])

    result = (wide + dot(attended, wproj[...])).astype(BF16)
    back_out = put_back(result, res, 0)

    for g in range(3):
        to_sib[2 + g].wait_recv()
    values_in = jnp.concatenate([agv_in[g, :, 128:256] for g in range(3)], 1)
    y_copies = [weight_part(0, hidden_own, hidden_in, grad_values, values_in)]
    to_sib[0].wait_recv()
    attended_in = own_half(jnp.concatenate([agv_in[g, :, 0:128] for g in range(3)], 1))
    y_copies.append(weight_part(1, attended_own, attended_in, cw[...], cw_in[...]))
    for g in range(3):
        lanes = slice(128 * g, 128 * g + 128)
        queries4 = jnp.concatenate([joined[:, lanes] * k for k in head_masks], 0)
        key_part = joined[:, 384 + 128 * g : 384 + 128 * g + 128]
        value_part = joined[:, 768 + 128 * g : 768 + 128 * g + 128]
        grad4 = jnp.concatenate([grad_att[:, lanes] * k for k in head_masks], 0)
        weights = probs[g]
        grad_probs = dot(grad4, value_part, 1, 1)
        grad_scores = weights * (grad_probs - jnp.sum(weights * grad_probs, 1, keepdims=True))
        for h in range(4):
            for m in range(6):
                row = 24 * (4 * g + h)
                gsb[m, row : row + 24, :] = grad_scores[144 * h + 24 * m : 144 * h + 24 * m + 24]
        grad_scaled = (grad_scores * SCALE).astype(BF16)
        grad_query = pick(dot(grad_scaled, key_part))
        grad_keys = dot(grad_scaled, queries4, 0, 0)
        gqk[g, :, 0:128] = grad_query.astype(BF16)
        gqk[g, :, 128:256] = grad_keys.astype(BF16)
        to_sib[5 + g].start()
        if g > 0:
            to_sib[4 + g].wait_recv()
            y_copies.append(weight_part(1 + g, hidden_own, hidden_in, gqk[g - 1], gqk_in[g - 1]))

    grad_joined = jnp.concatenate(
        [gqk[g, :, 128 * n : 128 * n + 128] for n in range(2) for g in range(3)] + [grad_values], 1
    )
    grad_hidden = dot(grad_joined, wqkv[...], 1, 1)
    grad_gain = jnp.sum(grad_hidden * normed, 0, keepdims=True)
    folded = dot(gsb[0].astype(BF16), toep[0])
    for m in range(1, 6):
        folded = folded + dot(gsb[m].astype(BF16), toep[m])
    folded = folded.astype(BF16)

    shares = dot(dup_t[0], folded[:, 0:384]) + dot(dup_t[1], folded[:, 384:768])
    share_row = lax.broadcasted_iota(jnp.int32, (16, 256), 0)
    share_lane = lax.broadcasted_iota(jnp.int32, (16, 256), 1)

    def riders(gain_row, kind_row):
        high = gain_row.astype(BF16).astype(F32)
        low = gain_row - high
        rows = [
            high[:, 0:256],
            jnp.concatenate([high[:, 256:384], jnp.zeros((1, 128), F32)], 1),
            low[:, 0:256],
            jnp.concatenate([low[:, 256:384], jnp.zeros((1, 128), F32)], 1),
        ]
        block = jnp.where((share_row == 15) & (share_lane >= 128), kind_row, 0.0)
        for n, row in enumerate(rows):
            block = block + jnp.where(share_row == 12 + n, row, 0.0)
        return block

    def gain_of(block):
        return jnp.concatenate(
            [block[12:13] + block[14:15], block[13:14, 0:128] + block[15:16, 0:128]], 1
        )

    extra = riders(grad_gain, kind.astype(F32))
    for dest in range(16):
        zp, zq, k = dest // 8, (dest // 4) % 2, dest % 4
        first = (6 * zp + 3 * k // 2) * 16
        edge = 69 if k % 2 else 138
        pieces = [
            roll_left(shares[row : row + 16], 138 * zq + start)[:, 0:256]
            for row, start in ((first, 138 - edge), (first + 16, -edge))
        ]
        block = jnp.where(share_lane < edge, *pieces)
        block = jnp.where((share_row < 12) & (share_lane < 207), block, 0.0) + extra
        bsend[dest] = block.astype(BF16)

    def bias_lon(d):
        to = (j + d) % 16
        return remote(bsend.at[to], brecv.at[d], b_s, b_r, (i, to))

    def start_all(make):
        def body(d, carry):
            make(d).start()
            return carry

        lax.fori_loop(1, 16, body, 0)

    all_lon = whole(lrecv.at[pl.ds(1, 15)], l_s, l_r)
    all_bias = whole(brecv.at[pl.ds(1, 15)], b_s, b_r)
    all_lat = whole(arecv.at[pl.ds(1, 15)], a_s, a_r)
    start_all(bias_lon)

    to_sib[7].wait_recv()
    y_copies.append(weight_part(4, hidden_own, hidden_in, gqk[2], gqk_in[2]))

    mine, to_x = over_x()
    grad_normed = grad_hidden * gain
    grad_wide = inv_std * (
        grad_normed
        - jnp.mean(grad_normed, 1, keepdims=True)
        - normed * jnp.mean(grad_normed * normed, 1, keepdims=True)
    )
    grad_in = (cot_rows.astype(F32) + grad_wide).astype(BF16)
    back_grad = put_back(grad_in, res_cot, 1)

    all_bias[1].wait()
    total = bsend[j].astype(F32)
    for d in range(1, 16):
        total = total + brecv[d].astype(F32)
    kinds = total[15:16, 128:129] * (1.0 / 16.0)
    block = jnp.where(share_row < 12, total, 0.0) + riders(gain_of(total), kinds)
    asend[...] = block.astype(BF16)

    def bias_lat(d):
        return remote(asend, arecv.at[d], a_s, a_r, ((i + d) % 16, j))

    start_all(bias_lat)

    own_qk = []
    for q in range(3):
        y_copies[2 + q][1].wait()
        chunk = zsend[q, 2 * y + x].astype(F32)
        for d in range(1, 8):
            chunk = chunk + zrecv[q, d].astype(F32)
        own_qk.append(chunk)
    to_x.wait_recv()
    got = xrecv[...].astype(F32)
    own_value = mine[0] + got[0:24]
    own_proj = mine[1] + got[24:48]
    own_qkv = jnp.concatenate(
        [part[0:24] for part in own_qk] + [part[24:48] for part in own_qk] + [own_value],
        1,
    )
    lane128 = lax.broadcasted_iota(jnp.int32, (24, 128), 1)
    for dest in range(16):
        off = 72 * dest
        a = min(off // 128 * 128, 896)
        piece = roll_left(own_qkv[:, a : a + 256], off - a)[:, :128]
        off = 24 * dest
        a = min(off // 128 * 128, 128)
        tail = roll_left(own_proj[:, a : a + 256], off - a - 72)[:, :128]
        block = jnp.where(lane128 < 72, piece, tail)
        block = jnp.concatenate([block, jnp.zeros((8, 128), F32)], 0)
        lsend[dest] = block.astype(BF16)

    def to_lon(d):
        to = (j + d) % 16
        return remote(lsend.at[to], lrecv.at[d], l_s, l_r, (i, to))

    start_all(to_lon)


    for c in (*halo, *to_sib, *back_out, *back_grad, to_x):
        c.wait_send()
    for sent, _ in y_copies:
        sent.wait()
    all_bias[0].wait()

    writes = []
    for n, (copies, target) in enumerate(((back_out, out_ref), (back_grad, gin_ref))):
        for c in copies:
            c.wait_recv()
        writes.append(pltpu.make_async_copy(landed[n], target, own_sem.at[2 + n]))
        writes[n].start()

    all_lat[1].wait()
    gain_total = jnp.zeros((1, 384), F32)
    sums = [jnp.zeros((16, 256), F32), jnp.zeros((16, 256), F32)]
    for d in range(16):
        block = asend[...] if d == 0 else arecv[d]
        block = block.astype(F32)
        gain_total = gain_total + gain_of(block)
        for t in range(2):
            hit = block[15:16, 128:129] == (2 * i + t).astype(F32)
            sums[t] = sums[t] + jnp.where(hit, block, 0.0)
    ggain_ref[...] = gain_total.reshape(384)
    for h in range(12):
        row = jnp.concatenate([sums[0][h : h + 1, 0:207], sums[1][h : h + 1, 0:207]], 0)
        gbias_ref[h] = row
    all_lat[0].wait()

    all_lon[1].wait()
    total = lsend[j].astype(F32)
    for d in range(1, 16):
        total = total + lrecv[d].astype(F32)
    gqkv_ref[...] = total[0:24, 0:72]
    gproj_ref[...] = roll_left(total[0:24], 72)[:, 0:24]
    all_lon[0].wait()
    for c in writes:
        c.wait()


def finish(*refs):
    for source, target in zip(refs[:6], refs[6:]):
        target[...] = source[...]


def local(inputs, cotangent, norm_gain, qkv_weight, proj_weight, bias_table, window_type, region):
    consts = patterns()
    vmem = pl.BlockSpec(memory_space=pltpu.VMEM)
    hbm = pl.BlockSpec(memory_space=pltpu.HBM)
    dma = pltpu.SemaphoreType.DMA
    tokens = (6, 12, 2, 384)
    shapes = [
        jax.ShapeDtypeStruct(tokens, BF16),
        jax.ShapeDtypeStruct(tokens, BF16),
        jax.ShapeDtypeStruct((384,), F32),
        jax.ShapeDtypeStruct((24, 72), F32),
        jax.ShapeDtypeStruct((24, 24), F32),
        jax.ShapeDtypeStruct((12, 2, 207), F32),
    ]
    outs = pl.pallas_call(
        kernel,
        out_shape=shapes,
        in_specs=[hbm] * 7 + [pl.BlockSpec(memory_space=pltpu.SMEM)] + [hbm] * len(consts),
        out_specs=[hbm] * 2 + [vmem] * 4,
        scratch_shapes=[
            pltpu.VMEM((384,), F32),
            pltpu.VMEM(qkv_weight.shape, BF16),
            pltpu.VMEM(proj_weight.shape, BF16),
            pltpu.VMEM((12, 32, 3312), BF16),
            pltpu.VMEM((6, 2, 12), jnp.int32),
        ]
        + [pltpu.VMEM(c.shape, BF16) for c in consts]
        + [
            pltpu.VMEM(tokens, BF16),
            pltpu.VMEM(tokens, BF16),
            pltpu.VMEM(tokens, BF16),
            pltpu.VMEM(tokens, BF16),
            pltpu.VMEM(tokens, BF16),
            pltpu.VMEM(tokens, BF16),
            pltpu.VMEM((144, 384), BF16),
            pltpu.VMEM((16, 128), F32),
            pltpu.VMEM((16, 3456), F32),
            pltpu.VMEM((192, 384), BF16),
            pltpu.VMEM((12, 144, 144), F32),
            pltpu.VMEM((3, 576, 144), F32),
            pltpu.VMEM((6, 288, 144), F32),
            pltpu.VMEM((3, 144, 256), BF16),
            pltpu.VMEM((3, 144, 256), BF16),
            pltpu.VMEM((144, 384), BF16),
            pltpu.VMEM((3, 144, 256), BF16),
            pltpu.VMEM((3, 144, 256), BF16),
            pltpu.VMEM((144, 384), BF16),
            pltpu.VMEM((144, 384), BF16),
            pltpu.VMEM((144, 384), BF16),
            pltpu.VMEM((2, 4, 48, 384), BF16),
            pltpu.VMEM((2, 4, 48, 384), BF16),
            pltpu.VMEM((3, 8, 48, 128), BF16),
            pltpu.VMEM((3, 8, 48, 128), BF16),
            pltpu.VMEM((48, 384), BF16),
            pltpu.VMEM((48, 384), BF16),
            pltpu.VMEM((16, 32, 128), BF16),
            pltpu.VMEM((16, 32, 128), BF16),
            pltpu.VMEM((16, 16, 256), BF16),
            pltpu.VMEM((16, 16, 256), BF16),
            pltpu.VMEM((16, 256), BF16),
            pltpu.VMEM((16, 16, 256), BF16),
            dma((len(consts) + 5,)), dma((4,)),
            dma((6,)), dma((6,)), dma((6,)), dma((6,)), dma((8,)), dma((8,)),
            dma((2,)), dma((2,)), dma((3,)), dma((3,)), dma, dma,
            dma, dma, dma, dma, dma, dma,
        ],
        compiler_params=pltpu.CompilerParams(
            collective_id=0, has_side_effects=True, vmem_limit_bytes=62 * 2**20
        ),
    )(
        inputs.transpose(1, 2, 0, 3),
        cotangent.transpose(1, 2, 0, 3),
        norm_gain,
        qkv_weight,
        proj_weight,
        bias_table.transpose(1, 0, 2),
        region.transpose(1, 0, 2),
        window_type,
        *consts,
    )
    outs = pl.pallas_call(
        finish,
        out_shape=shapes,
        in_specs=[vmem] * 6,
        out_specs=[vmem] * 6,
    )(*outs)
    block_out, grad_inputs, grad_gain, grad_qkv, grad_proj, grad_bias = outs
    return (
        block_out.transpose(2, 0, 1, 3),
        grad_inputs.transpose(2, 0, 1, 3),
        grad_gain,
        grad_qkv,
        grad_proj,
        grad_bias.transpose(1, 0, 2),
    )


def solution(mesh):
    return jax.shard_map(
        local,
        mesh=mesh,
        in_specs=(
            P(None, "lat", "lon", None),
            P(None, "lat", "lon", None),
            P(),
            P(),
            P(),
            P(),
            P("lat", None),
            P(None, "lat", "lon"),
        ),
        out_specs=(
            P(None, "lat", "lon", None),
            P(None, "lat", "lon", None),
            P(),
            P("lat", "lon"),
            P("lat", "lon"),
            P("lat", None, "lon"),
        ),
        check_vma=False,
    )
```
